32 devices in a mesh: rep: 4 (over y, x), fsdp: 8 (over z, core).
Axes of the slice: x: 2, y: 2, z: 4, core: 2. Of those that a mesh axis runs over, the one named last changes fastest.
Arguments:
- tokens: bfloat16 [4, 512, 8192], P('rep', None, 'fsdp'), may hold values from -6 to 6
- targets: bfloat16 [4, 512, 1024], P('rep', 'fsdp'), may hold values from -6 to 6
- inner_weights: float32 [4, 8192, 1024], P('rep', 'fsdp'), may hold values from -6 to 6
- outer_weights: float32 [8192, 1024], P('fsdp'), may hold values from -6 to 6
- outer_momentum: float32 [8192, 1024], P('fsdp'), may hold values from -3 to 3
- replica_weights: bfloat16 [4, 8192, 1024], P('rep', 'fsdp'), may hold values from -6 to 6
Outputs:
- new_inner: float32 [4, 8192, 1024], P('rep', 'fsdp')
- new_outer: float32 [8192, 1024], P('fsdp')
- new_moment: float32 [8192, 1024], P('fsdp')
- merged: bfloat16 [4, 8192, 1024], P('rep', 'fsdp')
The draws below stay inside these ranges and needn't reach their ends.
All inputs are finite; a program needn't handle non-finite values.
Results may differ from the reference program's by a relative error of at most 0.005.
Values may be sent and summed in bfloat16 or wider, within the bound.
No kernel may reach another device: no remote copies, remote signals or barrier semaphores. Data moves between devices by JAX's collectives and lax.ppermute only.
A program may use at most 64 MiB of HBM per device.

```python
import jax
import jax.numpy as jnp
from jax import lax

D = 8192
KV = 1024
TOK = 512
INNER = 2
REPS = 4


def levels(key, extent, pieces, low, largest):
    level, own = 1.0, jax.random.fold_in(key, 6)
    for position, parts in pieces:
        steps = jnp.exp(jax.random.uniform(jax.random.fold_in(own, position), (parts,), jnp.float32, low / len(pieces), largest / len(pieces)))
        level = level * jnp.repeat(steps, extent[position] // parts).reshape([-1 if axis == position else 1 for axis in range(len(extent))])
    return level


def gaussian(stream_key, shape, deviation, most, cuts=(), held_as=jnp.bfloat16):
    drawn = jax.random.normal(stream_key, shape, jnp.float32) * deviation
    if len(cuts) > 0:
        drawn = levels(stream_key, shape, cuts, -0.22, 0.18) * drawn
    return jnp.clip(drawn, min=-most, max=most).astype(held_as)


def setup_inputs(seed: int = 0) -> dict:
    seeds = jax.random.split(jax.random.key(seed), 7)
    tokens = gaussian(seeds[0], (REPS, TOK, D), 1.0, 6.0, ((0, 4), (2, 8)))
    targets = gaussian(seeds[1], (REPS, TOK, KV), 1.0, 6.0, ((0, 4), (1, 8)))
    inner_weights = gaussian(seeds[2], (REPS, D, KV), 1.0, 6.0, ((0, 4), (1, 8)), jnp.float32)
    outer_weights = gaussian(seeds[3], (D, KV), 1.0, 6.0, ((0, 8),), jnp.float32)
    outer_momentum = gaussian(seeds[4], (D, KV), 0.5, 3.0, ((0, 8),), jnp.float32)
    replica_weights = gaussian(seeds[5], (REPS, D, KV), 1.0, 6.0, ((0, 4), (1, 8)))
    return {"tokens": tokens, "targets": targets, "inner_weights": inner_weights, "outer_weights": outer_weights, "outer_momentum": outer_momentum, "replica_weights": replica_weights}


inner_rate = 0.5
momentum_coef = 0.9
outer_rate = 0.7
merge_keep = 0.5


def inner_steps(operands):
    token_rows, target_rows, weights_now = operands
    weight_scale = D ** -0.5
    for inner_turn in range(INNER):
        weights_half = weights_now.astype(jnp.bfloat16)
        predicted = jnp.dot(token_rows, weights_half, preferred_element_type=jnp.float32) * weight_scale
        errors = (predicted - target_rows.astype(jnp.float32)).astype(jnp.bfloat16)
        gradient = jnp.dot(token_rows.T, errors, preferred_element_type=jnp.float32) * weight_scale
        weights_now = weights_now - inner_rate * gradient
    return weights_now


def reference(tokens, targets, inner_weights, outer_weights, outer_momentum, replica_weights):
    new_inner = lax.map(inner_steps, (tokens, targets, inner_weights))

    def accumulate(carry, replica_rows):
        return carry + (outer_weights - replica_rows.astype(jnp.float32)), None

    pseudo_sum, unused = lax.scan(accumulate, jnp.zeros_like(outer_weights), replica_weights)
    outer_delta = pseudo_sum / REPS
    new_moment = momentum_coef * outer_momentum + outer_delta
    new_outer = outer_weights - outer_rate * (outer_delta + momentum_coef * new_moment)

    def merge_one(replica_rows):
        mixed = merge_keep * replica_rows.astype(jnp.float32) + (1.0 - merge_keep) * new_outer
        return mixed.astype(jnp.bfloat16)

    merged = lax.map(merge_one, replica_weights)
    return new_inner, new_outer, new_moment, merged
```

```python
import functools

import jax
import jax.numpy as jnp
from jax import lax
from jax.experimental import pallas as pl
from jax.experimental.pallas import tpu as pltpu
from jax.sharding import PartitionSpec as P

INNER = 2

inner_rate = 0.5
momentum_coef = 0.9
outer_rate = 0.7
merge_keep = 0.5

F32 = jnp.float32
BF16 = jnp.bfloat16
LANES = 128
MIB = 1 << 20

CODE_SCALE = 2.0**60
CODE_LEAST = 2.0**-30
CODE_CUT = 2.0**20


def encode(total, outer_rows, count):
    away = count * outer_rows - total
    held = jnp.where(jnp.abs(total) < CODE_LEAST, CODE_LEAST, total) * CODE_SCALE
    return jnp.where(jnp.abs(total) < jnp.abs(away), held, away).astype(BF16)


def decode_total(code, outer_rows, count):
    code = code.astype(F32)
    return jnp.where(jnp.abs(code) > CODE_CUT, code * (1.0 / CODE_SCALE), count * outer_rows - code)


def decode_away(code, outer_rows, count):
    code = code.astype(F32)
    return jnp.where(jnp.abs(code) > CODE_CUT, count * outer_rows - code * (1.0 / CODE_SCALE), code)


def swap(value, axis, flip):
    count = lax.axis_size(axis)
    return lax.ppermute(value, axis, [(i, i ^ flip) for i in range(count)])


def params(mib):
    return pltpu.CompilerParams(vmem_limit_bytes=mib * MIB)


def cost(flops, nbytes):
    return pl.CostEstimate(flops=int(flops), bytes_accessed=int(nbytes), transcendentals=0)


def row_slice(value, start, size):
    return lax.dynamic_slice_in_dim(value, start, size, 0)


def update_kernel(replicas, blocks, pos_ref, code_a, code_b, outer_ref, moment_ref, rep_ref, *rest):
    new_outer_ref, new_moment_ref, merged_ref = rest[-3:]
    step = pl.program_id(0)

    def update(code_ref):
        outer = outer_ref[...]
        delta = decode_away(code_ref[...], outer, float(replicas)) * (1.0 / replicas)
        moment = momentum_coef * moment_ref[...] + delta
        new_outer = outer - outer_rate * (delta + momentum_coef * moment)
        new_outer_ref[...] = new_outer
        new_moment_ref[...] = moment
        mixed = merge_keep * rep_ref[...].astype(F32) + (1.0 - merge_keep) * new_outer
        merged_ref[...] = mixed.astype(BF16)

    @pl.when(step < blocks)
    def _():
        update(code_a)

    @pl.when(step >= blocks)
    def _():
        update(code_b)


def outer_update(start_a, start_b, code_a, code_b, outer, moment, rep_rows, before):
    replicas = lax.axis_size("rep")
    size, width = code_a.shape
    block = min(size, 128)
    blocks = size // block
    pos = jnp.stack([start_a // block, start_b // block]).astype(jnp.int32)

    def at(i, pos_ref):
        return (jnp.where(i < blocks, pos_ref[0] + i, pos_ref[1] + i - blocks), 0)

    code_specs = [
        pl.BlockSpec((block, width), lambda i, pos_ref: (jnp.minimum(i, blocks - 1), 0)),
        pl.BlockSpec((block, width), lambda i, pos_ref: (jnp.maximum(i - blocks, 0), 0)),
    ]
    row_spec = pl.BlockSpec((block, width), at)
    rows = outer.shape[0]
    aliases = {} if before is None else {6: 0, 7: 1, 8: 2}
    held = () if before is None else before
    return pl.pallas_call(
        functools.partial(update_kernel, replicas, blocks),
        out_shape=(
            jax.ShapeDtypeStruct((rows, width), F32),
            jax.ShapeDtypeStruct((rows, width), F32),
            jax.ShapeDtypeStruct((rows, width), BF16),
        ),
        grid_spec=pltpu.PrefetchScalarGridSpec(
            num_scalar_prefetch=1,
            grid=(2 * blocks,),
            in_specs=code_specs + [row_spec] * 3 + [pl.BlockSpec(memory_space=pl.ANY)] * len(held),
            out_specs=[row_spec] * 3,
        ),
        input_output_aliases=aliases,
        compiler_params=params(16),
        cost_estimate=cost(20 * size * width, 2 * size * width * 22),
        name="outer_update",
    )(pos, code_a, code_b, outer, moment, rep_rows, *held)


def outer_sync(outer, moment, rep_rows):
    replicas = lax.axis_size("rep")
    index = lax.axis_index("rep")
    bits = replicas.bit_length() - 1
    rows = rep_rows.shape[0]
    half = rows // 2
    orders = (tuple(range(bits)), tuple(reversed(range(bits))))
    bases = (0, half)
    current = [rep_rows, rep_rows]
    offsets = [jnp.int32(0), jnp.int32(half)]
    starts = [jnp.int32(0), jnp.int32(half)]
    size = half
    count = 1
    for turn in range(bits):
        size //= 2
        sends, keeps = [], []
        for s in range(2):
            bit = (index >> orders[s][turn]) & 1
            send_at = (1 - bit) * size
            keep_at = bit * size
            send = row_slice(current[s], offsets[s] + send_at, size)
            keep = row_slice(current[s], offsets[s] + keep_at, size)
            if count > 1:
                send = encode(send, row_slice(outer, starts[s] + send_at, size), float(count))
            starts[s] = starts[s] + keep_at
            offsets[s] = jnp.int32(0)
            sends.append(send)
            keeps.append(keep)
        for s in range(2):
            got = swap(sends[s], "rep", 1 << orders[s][turn])
            if count > 1:
                got = decode_total(got, row_slice(outer, starts[s], size), float(count))
            current[s] = keeps[s].astype(F32) + got.astype(F32)
        count *= 2
    codes = [
        encode(current[s], row_slice(outer, starts[s], size), float(replicas)) for s in range(2)
    ]
    for turn in reversed(range(bits)):
        got = [swap(codes[s], "rep", 1 << orders[s][turn]) for s in range(2)]
        set_bits = [(index >> orders[s][turn]) & 1 for s in range(2)]
        low = [starts[s] - set_bits[s] * size for s in range(2)]
        if turn == 0:
            first = outer_update(starts[0], starts[1], codes[0], codes[1], outer, moment, rep_rows, None)
            far = [low[s] + (1 - set_bits[s]) * size for s in range(2)]
            return outer_update(far[0], far[1], got[0], got[1], outer, moment, rep_rows, first)
        for s in range(2):
            pair = jnp.where(
                set_bits[s] == 0,
                jnp.concatenate([codes[s], got[s]], 0),
                jnp.concatenate([got[s], codes[s]], 0),
            )
            codes[s] = pair
            starts[s] = low[s]
        size *= 2


def gram_kernel(scale, x_ref, keep_ref, send_ref, turned_ref, core_ref):
    x = x_ref[...]
    gram = lax.dot_general(x, x, (((1,), (1,)), ((), ())), preferred_element_type=F32) * scale
    tiles = x.shape[0] // LANES
    pairs = [(i, j) for i in range(tiles) for j in range(i, tiles)]
    each = len(pairs) // 2
    mine = core_ref[0]
    for place, (i, j) in enumerate(pairs):
        part = gram[i * LANES : (i + 1) * LANES, j * LANES : (j + 1) * LANES].astype(BF16)
        side, spot = place // each, place % each
        rows = pl.ds(spot * LANES, LANES)

        @pl.when(mine == side)
        def _():
            keep_ref[rows, :] = part

        @pl.when(mine != side)
        def _():
            send_ref[rows, :] = part

    turned_ref[...] = x.T


def gram_parts(x, core, scale):
    tokens, depth = x.shape
    tiles = tokens // LANES
    each = tiles * (tiles + 1) // 4
    vmem = pl.BlockSpec(memory_space=pltpu.VMEM)
    part = jax.ShapeDtypeStruct((each * LANES, LANES), BF16)
    return pl.pallas_call(
        lambda core_ref, x_ref, keep_ref, send_ref, turned_ref: gram_kernel(
            scale, x_ref, keep_ref, send_ref, turned_ref, core_ref
        ),
        out_shape=(part, part, jax.ShapeDtypeStruct((depth, tokens), BF16)),
        in_specs=[pl.BlockSpec(memory_space=pltpu.SMEM), vmem],
        out_specs=(vmem, vmem, vmem),
        compiler_params=params(16),
        cost_estimate=cost(2 * tokens * tokens * depth, 4 * tokens * depth),
        name="gram_parts",
    )(core, x)


def project_kernel(scale, info_ref, x_ref, w_ref, t_ref, out_ref, acc_ref):
    acc_ref[...] = scale * jnp.dot(x_ref[...], w_ref[...].astype(BF16), preferred_element_type=F32)
    own = t_ref.shape[0]
    rows = pl.ds(pl.multiple_of(info_ref[1] * own, own), own)
    acc_ref[rows, :] = acc_ref[rows, :] - t_ref[...].astype(F32)
    for piece in range(out_ref.shape[0]):
        out_ref[piece] = acc_ref[:, piece * LANES : (piece + 1) * LANES].astype(BF16)


def project(x, w, t, info, scale):
    tokens, depth = x.shape
    width = w.shape[1]
    span = 2 * LANES
    steps = width // 2 // span
    return pl.pallas_call(
        functools.partial(project_kernel, scale),
        out_shape=jax.ShapeDtypeStruct((width // 2 // LANES, tokens, LANES), BF16),
        grid_spec=pltpu.PrefetchScalarGridSpec(
            num_scalar_prefetch=1,
            grid=(steps,),
            in_specs=[
                pl.BlockSpec((tokens, depth), lambda j, info_ref: (0, 0)),
                pl.BlockSpec((depth, span), lambda j, info_ref: (0, info_ref[0] * steps + j)),
                pl.BlockSpec((t.shape[0], span), lambda j, info_ref: (0, info_ref[0] * steps + j)),
            ],
            out_specs=pl.BlockSpec((span // LANES, tokens, LANES), lambda j, info_ref: (j, 0, 0)),
            scratch_shapes=[pltpu.VMEM((tokens, span), F32)],
        ),
        compiler_params=params(16),
        cost_estimate=cost(tokens * depth * width, 2 * depth * width + 2 * tokens * depth),
        name="project",
    )(info, x, w, t)


def whole_gram_kernel(pos_ref, mine_ref, other_ref, out_ref, pack_ref):
    pieces, rows, _ = mine_ref.shape
    for spot in range(pieces):
        mine_at = pos_ref[spot] * rows
        other_at = pos_ref[pieces + spot] * rows
        pack_ref[pl.ds(pl.multiple_of(mine_at, rows), rows), :] = mine_ref[spot]
        pack_ref[pl.ds(pl.multiple_of(other_at, rows), rows), :] = other_ref[spot]
    tiles = out_ref.shape[0] // LANES
    pairs = [(i, j) for i in range(tiles) for j in range(i, tiles)]
    for place, (i, j) in enumerate(pairs):
        part = pack_ref[place * LANES : (place + 1) * LANES, :]
        out_ref[i * LANES : (i + 1) * LANES, j * LANES : (j + 1) * LANES] = part
        if i != j:
            out_ref[j * LANES : (j + 1) * LANES, i * LANES : (i + 1) * LANES] = part.T


def whole_gram(pos, mine, other, tokens):
    vmem = pl.BlockSpec(memory_space=pltpu.VMEM)
    pieces, rows, _ = mine.shape
    return pl.pallas_call(
        whole_gram_kernel,
        out_shape=jax.ShapeDtypeStruct((tokens, tokens), BF16),
        in_specs=[pl.BlockSpec(memory_space=pltpu.SMEM), vmem, vmem],
        out_specs=vmem,
        scratch_shapes=[pltpu.VMEM((2 * pieces * rows, LANES), BF16)],
        compiler_params=params(16),
        cost_estimate=cost(0, 4 * pieces * rows * LANES + 2 * tokens * tokens),
        name="whole_gram",
    )(pos, mine, other)


def residual_kernel(own_ref, *refs):
    got, gram_ref, out_ref = refs[:-2], refs[-2], refs[-1]
    error = own_ref[...].astype(F32)
    for ref in got:
        error = error + ref[...].astype(F32)
    moved = jnp.dot(gram_ref[...], error.astype(BF16), preferred_element_type=F32)
    out_ref[...] = (2.0 * error - moved).astype(BF16)


def residual(own, got, gram):
    vmem = pl.BlockSpec(memory_space=pltpu.VMEM)
    tokens, width = own.shape
    return pl.pallas_call(
        residual_kernel,
        out_shape=jax.ShapeDtypeStruct((tokens, width), BF16),
        in_specs=[vmem] * (2 + len(got)),
        out_specs=vmem,
        compiler_params=params(16),
        cost_estimate=cost(2 * tokens * tokens * width, 2 * tokens * (tokens + 5 * width)),
        name="residual",
    )(own, *got, gram)


def step_kernel(rate, pos_ref, turned_ref, *refs):
    out_ref = refs[-1]
    pieces, w_ref = refs[0], refs[1]
    grad = jnp.dot(turned_ref[...], pieces[0], preferred_element_type=F32)
    out_ref[...] = w_ref[...] - rate * grad


def weight_step(turned, pieces, pos, w, rate, before):
    depth, tokens = turned.shape
    count, _, width = pieces.shape
    held = () if before is None else (before,)
    return pl.pallas_call(
        functools.partial(step_kernel, rate),
        out_shape=jax.ShapeDtypeStruct(w.shape, F32),
        grid_spec=pltpu.PrefetchScalarGridSpec(
            num_scalar_prefetch=1,
            grid=(count,),
            in_specs=[
                pl.BlockSpec((depth, tokens), lambda j, pos_ref: (0, 0)),
                pl.BlockSpec((1, tokens, width), lambda j, pos_ref: (j, 0, 0)),
                pl.BlockSpec((depth, width), lambda j, pos_ref: (0, pos_ref[j])),
            ]
            + [pl.BlockSpec(memory_space=pl.ANY)] * len(held),
            out_specs=pl.BlockSpec((depth, width), lambda j, pos_ref: (0, pos_ref[j])),
        ),
        input_output_aliases={} if before is None else {4: 0},
        compiler_params=params(16),
        cost_estimate=cost(2 * tokens * depth * width * count, 8 * depth * width * count),
        name="weight_step",
    )(pos, turned, pieces, w, *held)


def inner_run(x, t, w):
    shards = lax.axis_size("fsdp")
    index = lax.axis_index("fsdp")
    core, chip = index & 1, index >> 1
    chips = shards // 2
    features = x.shape[1] * shards
    scale = features**-0.5
    tokens = x.shape[0]

    gram_keep, gram_send, turned = gram_parts(
        x, core.astype(jnp.int32)[None], inner_rate * scale * scale
    )
    gram_got = swap(gram_send, "fsdp", 1)

    def info(side):
        return jnp.stack([side, index]).astype(jnp.int32)

    error_send = project(x, w, t, info(1 - core), scale)
    error_got = swap(error_send, "fsdp", 1)
    error_keep = project(x, w, t, info(core), scale)

    def chip_sum(keep, got, place):
        return lax.dynamic_index_in_dim(keep, place, 0, False).astype(F32) + lax.dynamic_index_in_dim(
            got, place, 0, False
        ).astype(F32)

    def spread(keep, got):
        received = [
            swap(chip_sum(keep, got, chip ^ k).astype(BF16), "fsdp", 2 * k) for k in range(1, chips)
        ]
        return chip_sum(keep, got, chip), received

    def collect(piece):
        return jnp.stack([piece] + [swap(piece, "fsdp", 2 * k) for k in range(1, chips)])

    cut = (chips, gram_keep.shape[0] // chips, LANES)
    gram_own, gram_parts_got = spread(gram_keep.reshape(cut), gram_got.reshape(cut))
    for part in gram_parts_got:
        gram_own = gram_own + part.astype(F32)
    gram_mine = collect(gram_own.astype(BF16))
    gram_other = swap(gram_mine, "fsdp", 1)
    mine_at = jnp.stack([core * chips + (chip ^ k) for k in range(chips)]).astype(jnp.int32)
    other_at = jnp.stack([(1 - core) * chips + (chip ^ k) for k in range(chips)]).astype(jnp.int32)
    gram = whole_gram(jnp.concatenate([mine_at, other_at]), gram_mine, gram_other, tokens)

    error_own, error_parts = spread(error_keep, error_got)
    moved = residual(error_own, error_parts, gram)
    mine = collect(moved)
    other = swap(mine, "fsdp", 1)
    first = weight_step(turned, mine, mine_at, w, inner_rate * scale, None)
    return weight_step(turned, other, other_at, w, inner_rate * scale, first)


def plain_outer(outer, moment, rep_rows):
    replica_rows = rep_rows.astype(F32)
    delta = lax.psum(outer - replica_rows, "rep") / lax.axis_size("rep")
    new_moment = momentum_coef * moment + delta
    new_outer = outer - outer_rate * (delta + momentum_coef * new_moment)
    mixed = merge_keep * replica_rows + (1.0 - merge_keep) * new_outer
    return new_outer, new_moment, mixed.astype(BF16)


def plain_inner(x, t, w):
    scale = (x.shape[1] * lax.axis_size("fsdp")) ** -0.5
    for _ in range(INNER):
        part = jnp.dot(x, w.astype(BF16), preferred_element_type=F32).astype(BF16)
        predicted = lax.psum_scatter(part, "fsdp", scatter_dimension=0, tiled=True).astype(F32) * scale
        errors = lax.all_gather((predicted - t.astype(F32)).astype(BF16), "fsdp", axis=0, tiled=True)
        gradient = lax.dot_general(x, errors, (((0,), (0,)), ((), ())), preferred_element_type=F32)
        w = w - inner_rate * scale * gradient
    return w


def power_of_two(value):
    return value > 1 and value & (value - 1) == 0


def local(tokens, targets, inner_weights, outer_weights, outer_momentum, replica_weights):
    x, t, w, rep_rows = tokens[0], targets[0], inner_weights[0], replica_weights[0]
    replicas, shards = lax.axis_size("rep"), lax.axis_size("fsdp")
    if power_of_two(replicas) and rep_rows.shape[0] % (32 * replicas) == 0:
        new_outer, new_moment, merged = outer_sync(outer_weights, outer_momentum, rep_rows)
    else:
        new_outer, new_moment, merged = plain_outer(outer_weights, outer_momentum, rep_rows)
    tiles = x.shape[0] // LANES
    if (
        power_of_two(shards)
        and w.shape[1] == shards * LANES
        and x.shape[0] % LANES == 0
        and tiles * (tiles + 1) // 2 * LANES % (16 * shards) == 0
    ):
        new_inner = inner_run(x, t, w)
    else:
        new_inner = plain_inner(x, t, w)
    return new_inner[None], new_outer, new_moment, merged[None]


def solution(mesh):
    placed = (
        P("rep", None, "fsdp"),
        P("rep", "fsdp", None),
        P("rep", "fsdp", None),
        P("fsdp", None),
        P("fsdp", None),
        P("rep", "fsdp", None),
    )
    return jax.shard_map(
        local,
        mesh=mesh,
        in_specs=placed,
        out_specs=(
            P("rep", "fsdp", None),
            P("fsdp", None),
            P("fsdp", None),
            P("rep", "fsdp", None),
        ),
        check_vma=False,
    )
```

```python
import functools

import jax
import jax.numpy as jnp
from jax import lax
from jax.experimental import pallas as pl
from jax.experimental.pallas import tpu as pltpu
from jax.sharding import PartitionSpec as P

INNER = 2

inner_rate = 0.5
momentum_coef = 0.9
outer_rate = 0.7
merge_keep = 0.5

F32 = jnp.float32
BF16 = jnp.bfloat16
LANES = 128
SPAN = 2 * LANES
MIB = 1 << 20

CODE_SCALE = 2.0**60
CODE_LEAST = 2.0**-30
CODE_CUT = 2.0**20


WEIGHT = {
    "opening": 4,
    "project": 1,
    "add_1": 0,
    "add_2": 0,
    "add_3": 0,
    "fold_1": 0,
    "fold_2": 400,
    "code_1": 0,
    "code_2": 0,
    "code_3": 0,
    "code_4": 0,
    "whole_gram": 0,
    "residual": 0,
    "near_update": 40,
    "weight_step": 10,
    "far_update": 10,
}


def encode(total, outer_rows, count):
    away = count * outer_rows - total
    held = jnp.where(jnp.abs(total) < CODE_LEAST, CODE_LEAST, total) * CODE_SCALE
    return jnp.where(jnp.abs(total) < jnp.abs(away), held, away).astype(BF16)


def decode_total(code, outer_rows, count):
    code = code.astype(F32)
    return jnp.where(jnp.abs(code) > CODE_CUT, code * (1.0 / CODE_SCALE), count * outer_rows - code)


def decode_away(code, outer_rows, count):
    code = code.astype(F32)
    return jnp.where(jnp.abs(code) > CODE_CUT, count * outer_rows - code * (1.0 / CODE_SCALE), code)


def swap(value, axis, flip):
    count = lax.axis_size(axis)
    return lax.ppermute(value, axis, [(i, i ^ flip) for i in range(count)])


VMEM = pl.BlockSpec(memory_space=pltpu.VMEM)
HBM = pl.BlockSpec(memory_space=pl.ANY)
SMEM = pl.BlockSpec(memory_space=pltpu.SMEM)


def in_hbm(value):
    return pltpu.with_memory_space_constraint(value, pltpu.HBM)


def near(shape, dtype):
    return pltpu.VMEM(tuple(shape), dtype)


def far(shape, dtype):
    return pltpu.HBM(tuple(shape), dtype)


def run(kernel, outs, ins, copies, scratch=(), weight=0, mib=8, aliases=None, name="kernel"):
    specs = [spec for _, spec in ins]
    return pl.pallas_call(
        kernel,
        out_shape=tuple(outs),
        in_specs=specs,
        out_specs=tuple(VMEM if out.memory_space == pltpu.VMEM else HBM for out in outs),
        scratch_shapes=list(scratch) + ([pltpu.SemaphoreType.DMA((copies,))] if copies else []),
        input_output_aliases=aliases or {},
        compiler_params=pltpu.CompilerParams(vmem_limit_bytes=mib * MIB),
        cost_estimate=pl.CostEstimate(flops=0, bytes_accessed=weight * MIB, transcendentals=0),
        name=name,
    )(*[value for value, _ in ins])


def rows_at(block, size):
    return pl.ds(pl.multiple_of(block * size, size), size)


CORE, SHARD, CHIP_BIT_0, CHIP_BIT_1, KEEP_A, SEND_A, KEEP_B, SEND_B, CHIP = range(9)


def positions(quarters):
    shard, rep = lax.axis_index("fsdp"), lax.axis_index("rep")
    chip = shard >> 1
    bit_a, bit_b = rep & 1, (rep >> 1) & 1
    return jnp.stack(
        [shard & 1, shard, chip & 1, (chip >> 1) & 1, bit_a, 1 - bit_a, 2 + bit_b, 3 - bit_b, chip]
    ).astype(jnp.int32)


def open_kernel(scale, pos_ref, x_ref, rep_ref, keep_ref, send_ref, x_out, first_a, first_b, sems):
    quarter = first_a.shape[0]
    copy_x = pltpu.make_async_copy(x_ref, x_out, sems.at[0])
    copy_a = pltpu.make_async_copy(rep_ref.at[rows_at(pos_ref[SEND_A], quarter)], first_a, sems.at[1])
    copy_b = pltpu.make_async_copy(rep_ref.at[rows_at(pos_ref[SEND_B], quarter)], first_b, sems.at[2])
    copy_x.start()
    copy_a.start()
    copy_b.start()
    copy_x.wait()
    x = x_out[...]
    gram = lax.dot_general(x, x, (((1,), (1,)), ((), ())), preferred_element_type=F32) * scale
    tiles = x.shape[0] // LANES
    pairs = [(i, j) for i in range(tiles) for j in range(i, tiles)]
    each = len(pairs) // 2
    mine = pos_ref[CORE]
    for place, (i, j) in enumerate(pairs):
        part = gram[i * LANES : (i + 1) * LANES, j * LANES : (j + 1) * LANES].astype(BF16)
        side, spot = place // each, place % each
        rows = pl.ds(spot * LANES, LANES)

        @pl.when(mine == side)
        def _():
            keep_ref[rows, :] = part

        @pl.when(mine != side)
        def _():
            send_ref[rows, :] = part

    copy_a.wait()
    copy_b.wait()


def opening(pos, x, rep_rows, scale):
    tokens, depth = x.shape
    tiles = tokens // LANES
    each = tiles * (tiles + 1) // 4 * LANES
    quarter = (rep_rows.shape[0] // 4, rep_rows.shape[1])
    return run(
        functools.partial(open_kernel, scale),
        [near((each, LANES), BF16)] * 2 + [near(x.shape, BF16)] + [near(quarter, BF16)] * 2,
        [(pos, SMEM), (in_hbm(x), HBM), (in_hbm(rep_rows), HBM)],
        3,
        weight=WEIGHT["opening"],
        name="opening",
    )


def reversed_bits(value, bits):
    return sum(((value >> bit) & 1) << (bits - 1 - bit) for bit in range(bits))


def project_kernel(
    scale, pos_ref, x_ref, t_hbm, w_ref, rep_ref, outer_ref, keep_ref, *refs
):
    sends, (w_out, rep_a, rep_b, outer_a, outer_b, acc_ref, t_ref, sems) = refs[:-8], refs[-8:]
    steps = keep_ref.shape[0]
    bits = steps.bit_length() - 1
    quarter = rep_a.shape[0]
    copy_t = pltpu.make_async_copy(t_hbm, t_ref, sems.at[steps + 4])
    copy_t.start()
    copies = []
    for j in range(steps):
        place = reversed_bits(j, bits)
        copy = pltpu.make_async_copy(w_ref.at[:, pl.ds(place * SPAN, SPAN)], w_out.at[place], sems.at[j])
        copy.start()
        copies.append(copy)
    others = []
    for k, (source, entry, target) in enumerate(
        [(rep_ref, KEEP_A, rep_a), (rep_ref, KEEP_B, rep_b), (outer_ref, KEEP_A, outer_a), (outer_ref, KEEP_B, outer_b)]
    ):
        copy = pltpu.make_async_copy(source.at[rows_at(pos_ref[entry], quarter)], target, sems.at[steps + k])
        copy.start()
        others.append(copy)
    own = t_ref.shape[0]
    rows = rows_at(pos_ref[SHARD], own)
    copy_t.wait()
    for j in range(steps):
        place = reversed_bits(j, bits)
        copies[j].wait()
        acc_ref[...] = scale * jnp.dot(x_ref[...], w_out[place].astype(BF16), preferred_element_type=F32)
        acc_ref[rows, :] = acc_ref[rows, :] - t_ref[:, place * SPAN : (place + 1) * SPAN].astype(F32)
        for side in range(2):

            @pl.when(pos_ref[CORE] == side)
            def _():
                keep_ref[j] = acc_ref[:, side * LANES : (side + 1) * LANES].astype(BF16)

            @pl.when(pos_ref[CORE] != side)
            def _():
                sends[j][...] = acc_ref[:, side * LANES : (side + 1) * LANES].astype(BF16)

    for copy in others:
        copy.wait()


def project(pos, x, t, w, rep_rows, outer, scale):
    tokens, depth = x.shape
    steps = w.shape[1] // SPAN
    quarter = (rep_rows.shape[0] // 4, rep_rows.shape[1])
    return run(
        functools.partial(project_kernel, scale),
        [near((steps, tokens, LANES), BF16)]
        + [near((tokens, LANES), BF16)] * steps
        + [near((steps, depth, SPAN), F32)]
        + [near(quarter, BF16)] * 2
        + [near(quarter, F32)] * 2,
        [(pos, SMEM), (x, VMEM), (in_hbm(t), HBM), (in_hbm(w), HBM), (in_hbm(rep_rows), HBM), (in_hbm(outer), HBM)],
        steps + 5,
        scratch=[pltpu.VMEM((tokens, SPAN), F32), pltpu.VMEM(t.shape, BF16)],
        weight=WEIGHT["project"],
        name="project",
    )


def fold_kernel(entry, pos_ref, own_ref, *refs):
    gots, leave_ref, stay_ref = refs[:-2], refs[-2], refs[-1]
    size = stay_ref.shape[0]
    each = own_ref.shape[0] // len(gots)

    def total(place):
        got = gots[place // each]
        got = got[...] if each == 1 and len(got.shape) == 2 else got[place % each]
        return own_ref[place].astype(F32) + got.astype(F32)

    for side in range(2):

        @pl.when(pos_ref[entry] == side)
        def _():
            for k in range(size):
                leave_ref[k] = total((1 - side) * size + k).astype(BF16)
                stay_ref[k] = total(side * size + k)


def fold(pos, own, gots, entry, weight):
    size, tokens, width = own.shape
    shape = (size // 2, tokens, width)
    return run(
        functools.partial(fold_kernel, entry),
        [near(shape, BF16), near(shape, F32)],
        [(pos, SMEM), (own, VMEM)] + [(got, VMEM) for got in gots],
        0,
        weight=weight,
        name="fold",
    )


def add_kernel(own_ref, got_ref, out_ref):
    out_ref[...] = (own_ref[...].astype(F32) + got_ref[...].astype(F32)).astype(BF16)


def add(own, got, weight):
    return run(
        add_kernel,
        [near(own.shape, BF16)],
        [(own, VMEM), (got, VMEM)],
        0,
        weight=weight,
        name="add",
    )[0]


def whole_gram_kernel(pos_ref, x_ref, mine_ref, other_ref, out_ref, turned_ref):
    tiles = out_ref.shape[0] // LANES
    pairs = [(i, j) for i in range(tiles) for j in range(i, tiles)]
    each = len(pairs) // 2
    mine_first = pos_ref[CORE] == 0
    for place, (i, j) in enumerate(pairs):
        rows = pl.ds((place % each) * LANES, LANES)
        here = mine_first if place < each else jnp.logical_not(mine_first)
        part = jnp.where(here, mine_ref[rows, :], other_ref[rows, :])
        out_ref[i * LANES : (i + 1) * LANES, j * LANES : (j + 1) * LANES] = part
        if i != j:
            out_ref[j * LANES : (j + 1) * LANES, i * LANES : (i + 1) * LANES] = part.T
    turned_ref[...] = x_ref[...].T


def whole_gram(pos, x, mine, other):
    tokens, depth = x.shape
    return run(
        whole_gram_kernel,
        [near((tokens, tokens), BF16), near((depth, tokens), BF16)],
        [(pos, SMEM), (x, VMEM), (mine, VMEM), (other, VMEM)],
        0,
        weight=WEIGHT["whole_gram"],
        name="whole_gram",
    )


def residual_kernel(own_ref, got_ref, gram_ref, out_ref):
    error = own_ref[0] + got_ref[0].astype(F32)
    moved = jnp.dot(gram_ref[...], error.astype(BF16), preferred_element_type=F32)
    out_ref[...] = (2.0 * error - moved).astype(BF16)


def residual(own, got, gram):
    _, tokens, width = own.shape
    return run(
        residual_kernel,
        [near((tokens, width), BF16)],
        [(own, VMEM), (got, VMEM), (gram, VMEM)],
        0,
        weight=WEIGHT["residual"],
        name="residual",
    )[0]


def step_kernel(rate, places, pos_ref, turned_ref, w_ref, *refs):
    count = len(places)
    pieces = refs[: 2 * count]
    out_ref, pair_ref, buffer_ref, sems = refs[-4:]
    first = pos_ref[CORE] == 0
    copies = []
    for k, flip in enumerate(places):
        mine, other = pieces[2 * k][...], pieces[2 * k + 1][...]
        pair_ref[:, :LANES] = jnp.where(first, mine, other)
        pair_ref[:, LANES:] = jnp.where(first, other, mine)
        place = jnp.bitwise_xor(pos_ref[CHIP], flip)
        grad = jnp.dot(turned_ref[...], pair_ref[...], preferred_element_type=F32)
        buffer_ref[k] = w_ref[place] - rate * grad
        copy = pltpu.make_async_copy(
            buffer_ref.at[k], out_ref.at[:, pl.ds(pl.multiple_of(place * SPAN, SPAN), SPAN)], sems.at[k]
        )
        copy.start()
        copies.append(copy)
    for copy in copies:
        copy.wait()


def weight_step(pos, turned, w, pairs, places, rate, before):
    depth, tokens = turned.shape
    count = len(pairs)
    flat = [piece for pair in pairs for piece in pair]
    ins = [(pos, SMEM), (turned, VMEM), (w, VMEM)] + [(piece, VMEM) for piece in flat]
    aliases = {}
    if before is not None:
        aliases = {len(ins): 0}
        ins.append((before, HBM))
    return run(
        functools.partial(step_kernel, rate, tuple(places)),
        [far((depth, w.shape[0] * SPAN), F32)],
        ins,
        count,
        scratch=[pltpu.VMEM((tokens, SPAN), BF16), pltpu.VMEM((count, depth, SPAN), F32)],
        aliases=aliases,
        weight=WEIGHT["weight_step"],
        name="weight_step",
    )[0]


def first_code_kernel(rep_ref, got_ref, outer_ref, code_ref):
    total = rep_ref[...].astype(F32) + got_ref[...].astype(F32)
    code_ref[...] = encode(total, outer_ref[...], 2.0)


def second_code_kernel(own_ref, got_ref, outer_ref, code_ref):
    outer = outer_ref[...]
    total = decode_total(own_ref[...], outer, 2.0) + decode_total(got_ref[...], outer, 2.0)
    code_ref[...] = encode(total, outer, 4.0)


def code(kernel, own, got, outer_rows, weight):
    return run(
        kernel,
        [near(own.shape, BF16)],
        [(own, VMEM), (got, VMEM), (outer_rows, VMEM)],
        0,
        weight=weight,
        name="code",
    )[0]


PART = 128


def update_rows(entries, pos_ref, codes, outers, moments, reps, outs, buffers, sems, ready):
    size = codes[0].shape[0]
    copies = []
    part = min(PART, size)
    for half in range(2):
        for cut in range(size // part):
            spot = half * (size // part) + cut
            rows = pl.ds(cut * part, part)
            here = pl.ds(spot * part, part)
            if cut == 0:
                ready(half)
            outer = outers[half][rows, :]
            delta = decode_away(codes[half][rows, :], outer, 4.0) * 0.25
            moment = momentum_coef * moments[half][rows, :] + delta
            new_outer = outer - outer_rate * (delta + momentum_coef * moment)
            mixed = merge_keep * reps[half][rows, :].astype(F32) + (1.0 - merge_keep) * new_outer
            for k, value in enumerate((new_outer, moment, mixed.astype(BF16))):
                buffers[k][here, :] = value
                target = rows_at(pos_ref[entries[half]] * (size // part) + cut, part)
                copy = pltpu.make_async_copy(buffers[k].at[here], outs[k].at[target], sems.at[3 * spot + k])
                copy.start()
                copies.append(copy)
    for copy in copies:
        copy.wait()


def near_update_kernel(
    pos_ref, code_a, code_b, outer_a, outer_b, rep_a, rep_b, outer_ref, moment_ref, rep_ref,
    new_outer, new_moment, merged, far_outer_a, far_outer_b, far_moment_a, far_moment_b, far_rep_a, far_rep_b,
    moment_a, moment_b, buffer_outer, buffer_moment, buffer_merged, sems,
):
    size = code_a.shape[0]
    base = 6 * max(size // PART, 1)
    fetches = [
        (moment_ref, KEEP_A, moment_a),
        (moment_ref, KEEP_B, moment_b),
        (outer_ref, SEND_A, far_outer_a),
        (outer_ref, SEND_B, far_outer_b),
        (moment_ref, SEND_A, far_moment_a),
        (moment_ref, SEND_B, far_moment_b),
        (rep_ref, SEND_A, far_rep_a),
        (rep_ref, SEND_B, far_rep_b),
    ]
    copies = []
    for k, (source, entry, target) in enumerate(fetches):
        copy = pltpu.make_async_copy(source.at[rows_at(pos_ref[entry], size)], target, sems.at[base + k])
        copy.start()
        copies.append(copy)
    update_rows(
        (KEEP_A, KEEP_B), pos_ref, (code_a, code_b), (outer_a, outer_b), (moment_a, moment_b), (rep_a, rep_b),
        (new_outer, new_moment, merged), (buffer_outer, buffer_moment, buffer_merged), sems,
        lambda half: copies[half].wait(),
    )
    for copy in copies[2:]:
        copy.wait()


def far_update_kernel(
    pos_ref, code_a, code_b, outer_a, outer_b, moment_a, moment_b, rep_a, rep_b, held_a, held_b, held_c,
    new_outer, new_moment, merged, buffer_outer, buffer_moment, buffer_merged, sems,
):
    del held_a, held_b, held_c
    update_rows(
        (SEND_A, SEND_B), pos_ref, (code_a, code_b), (outer_a, outer_b), (moment_a, moment_b), (rep_a, rep_b),
        (new_outer, new_moment, merged), (buffer_outer, buffer_moment, buffer_merged), sems,
        lambda half: None,
    )


def update_scratch(size, width):
    return [pltpu.VMEM((2 * size, width), dtype) for dtype in (F32, F32, BF16)]


def near_update(pos, codes, outers, reps, outer, moment, rep_rows):
    size, width = codes[0].shape
    full = outer.shape
    return run(
        near_update_kernel,
        [far(full, F32), far(full, F32), far(full, BF16)]
        + [near((size, width), F32)] * 4
        + [near((size, width), BF16)] * 2,
        [(pos, SMEM)]
        + [(value, VMEM) for value in (*codes, *outers, *reps)]
        + [(in_hbm(value), HBM) for value in (outer, moment, rep_rows)],
        6 * max(size // PART, 1) + 8,
        scratch=[pltpu.VMEM((size, width), F32)] * 2 + update_scratch(size, width),
        mib=16,
        weight=WEIGHT["near_update"],
        name="near_update",
    )


def far_update(pos, codes, fetched, before):
    size, width = codes[0].shape
    outs = [far(value.shape, value.dtype) for value in before]
    ins = [(pos, SMEM)] + [(value, VMEM) for value in (*codes, *fetched)]
    return run(
        far_update_kernel,
        outs,
        ins + [(value, HBM) for value in before],
        6 * max(size // PART, 1),
        scratch=update_scratch(size, width),
        mib=16,
        aliases={len(ins) + k: k for k in range(3)},
        weight=WEIGHT["far_update"],
        name="far_update",
    )


def after(value, *others):
    return lax.optimization_barrier((value, *others))[0]


def both(x, t, w, outer, moment, rep_rows):
    shards = lax.axis_size("fsdp")
    chips = shards // 2
    scale = (x.shape[1] * shards) ** -0.5
    pos = positions(4)

    gram_keep, gram_send, x, first_a, first_b = opening(pos, x, rep_rows, inner_rate * scale * scale)
    gram_got = swap(gram_send, "fsdp", 1)
    got_a, got_b = swap(first_a, "rep", 1), swap(first_b, "rep", 2)
    gram_1 = add(gram_keep, gram_got, WEIGHT["add_1"])
    gram_got = swap(gram_1, "fsdp", 2)

    keep, *refs = project(after(pos, gram_1), x, t, w, rep_rows, outer, scale)
    sends, (w, rep_a, rep_b, outer_a, outer_b) = refs[:-5], refs[-5:]
    gram_2 = add(after(gram_1, keep), gram_got, WEIGHT["add_2"])
    gram_got = swap(gram_2, "fsdp", 4)
    got = [swap(send, "fsdp", 1) for send in sends]
    leave_1, stay = fold(pos, after(keep, gram_2), got, CHIP_BIT_0, WEIGHT["fold_1"])
    got = swap(leave_1, "fsdp", 2)

    code_a = code(first_code_kernel, after(rep_a, leave_1), got_a, outer_a, WEIGHT["code_1"])
    got_a = swap(code_a, "rep", 2)
    code_b = code(first_code_kernel, after(rep_b, code_a), got_b, outer_b, WEIGHT["code_2"])
    got_b = swap(code_b, "rep", 1)

    leave_2, stay = fold(pos, after(stay, code_b), [got], CHIP_BIT_1, WEIGHT["fold_2"])
    got = swap(leave_2, "fsdp", 4)
    gram = add(after(gram_2, leave_2), gram_got, WEIGHT["add_3"])
    pieces = [gram[: gram.shape[0] // 2], gram[gram.shape[0] // 2 :]]
    gram_got = [swap(piece, "fsdp", 1) for piece in pieces]

    code_a = code(second_code_kernel, after(code_a, gram), got_a, outer_a, WEIGHT["code_3"])
    got_a = swap(code_a, "rep", 1)
    code_b = code(second_code_kernel, after(code_b, code_a), got_b, outer_b, WEIGHT["code_4"])
    got_b = swap(code_b, "rep", 2)

    gram, turned = whole_gram(after(pos, code_b), x, gram, jnp.concatenate(gram_got, 0))
    moved = residual(stay, got, gram)
    updated = near_update(
        after(pos, moved), (code_a, code_b), (outer_a, outer_b), (rep_a, rep_b), outer, moment, rep_rows
    )
    mine = [moved] + [swap(moved, "fsdp", 2 * k) for k in range(1, chips)]
    pairs = [(piece, swap(after(piece, updated[0]), "fsdp", 1)) for piece in mine]
    result = weight_step(pos, turned, w, pairs, range(chips), inner_rate * scale, None)
    outers = far_update(after(pos, result), (got_a, got_b), updated[3:], updated[:3])
    return result, *outers


def plain_outer(outer, moment, rep_rows):
    replica_rows = rep_rows.astype(F32)
    delta = lax.psum(outer - replica_rows, "rep") / lax.axis_size("rep")
    new_moment = momentum_coef * moment + delta
    new_outer = outer - outer_rate * (delta + momentum_coef * new_moment)
    mixed = merge_keep * replica_rows + (1.0 - merge_keep) * new_outer
    return new_outer, new_moment, mixed.astype(BF16)


def plain_inner(x, t, w):
    scale = (x.shape[1] * lax.axis_size("fsdp")) ** -0.5
    for _ in range(INNER):
        part = jnp.dot(x, w.astype(BF16), preferred_element_type=F32).astype(BF16)
        predicted = lax.psum_scatter(part, "fsdp", scatter_dimension=0, tiled=True).astype(F32) * scale
        errors = lax.all_gather((predicted - t.astype(F32)).astype(BF16), "fsdp", axis=0, tiled=True)
        gradient = lax.dot_general(x, errors, (((0,), (0,)), ((), ())), preferred_element_type=F32)
        w = w - inner_rate * scale * gradient
    return w


def local(tokens, targets, inner_weights, outer_weights, outer_momentum, replica_weights):
    x, t, w, rep_rows = tokens[0], targets[0], inner_weights[0], replica_weights[0]
    tiles = x.shape[0] // LANES
    if (
        lax.axis_size("fsdp") == 8
        and lax.axis_size("rep") == 4
        and w.shape[1] == 8 * LANES
        and x.shape[0] % LANES == 0
        and tiles * (tiles + 1) % 4 == 0
        and rep_rows.shape[0] % (4 * PART) == 0
    ):
        new_inner, new_outer, new_moment, merged = both(x, t, w, outer_weights, outer_momentum, rep_rows)
    else:
        new_outer, new_moment, merged = plain_outer(outer_weights, outer_momentum, rep_rows)
        new_inner = plain_inner(x, t, w)
    return new_inner[None], new_outer, new_moment, merged[None]


def solution(mesh):
    placed = (
        P("rep", None, "fsdp"),
        P("rep", "fsdp", None),
        P("rep", "fsdp", None),
        P("fsdp", None),
        P("fsdp", None),
        P("rep", "fsdp", None),
    )
    return jax.shard_map(
        local,
        mesh=mesh,
        in_specs=placed,
        out_specs=(
            P("rep", "fsdp", None),
            P("fsdp", None),
            P("fsdp", None),
            P("rep", "fsdp", None),
        ),
        check_vma=False,
    )
```

```python
import functools

import jax
import jax.numpy as jnp
from jax import lax
from jax.experimental import pallas as pl
from jax.experimental.pallas import tpu as pltpu
from jax.sharding import PartitionSpec as P

INNER = 2

inner_rate = 0.5
momentum_coef = 0.9
outer_rate = 0.7
merge_keep = 0.5

F32 = jnp.float32
BF16 = jnp.bfloat16
LANES = 128
SPAN = 2 * LANES
MIB = 1 << 20
US = 1150000000

CODE_SCALE = 2.0**60
CODE_LEAST = 2.0**-30
CODE_CUT = 2.0**20


WEIGHT = {
    "opening": 1,
    "fetch": 0,
    "add_1": 0,
    "add_2": 20,
    "add_3": 20,
    "fold_1": 20,
    "fold_2": 8,
    "code_1": 0,
    "code_2": 0,
    "code_3": 0,
    "code_4": 0,
    "whole_gram": 0,
    "residual": 0,
    "near_update": 20,
    "weight_step": 0,
    "far_update": 0,
}


def encode(total, outer_rows, count):
    away = count * outer_rows - total
    held = jnp.where(jnp.abs(total) < CODE_LEAST, CODE_LEAST, total) * CODE_SCALE
    return jnp.where(jnp.abs(total) < jnp.abs(away), held, away).astype(BF16)


def decode_total(code, outer_rows, count):
    code = code.astype(F32)
    return jnp.where(jnp.abs(code) > CODE_CUT, code * (1.0 / CODE_SCALE), count * outer_rows - code)


def decode_away(code, outer_rows, count):
    code = code.astype(F32)
    return jnp.where(jnp.abs(code) > CODE_CUT, count * outer_rows - code * (1.0 / CODE_SCALE), code)


def swap(value, axis, flip):
    count = lax.axis_size(axis)
    return lax.ppermute(value, axis, [(i, i ^ flip) for i in range(count)])


VMEM = pl.BlockSpec(memory_space=pltpu.VMEM)
HBM = pl.BlockSpec(memory_space=pl.ANY)
SMEM = pl.BlockSpec(memory_space=pltpu.SMEM)


def in_hbm(value):
    return pltpu.with_memory_space_constraint(value, pltpu.HBM)


def near(shape, dtype):
    return pltpu.VMEM(tuple(shape), dtype)


def far(shape, dtype):
    return pltpu.HBM(tuple(shape), dtype)


def run(kernel, outs, ins, copies, scratch=(), weight=0, mib=8, aliases=None, name="kernel"):
    specs = [spec for _, spec in ins]
    return pl.pallas_call(
        kernel,
        out_shape=tuple(outs),
        in_specs=specs,
        out_specs=tuple(VMEM if out.memory_space == pltpu.VMEM else HBM for out in outs),
        scratch_shapes=list(scratch) + ([pltpu.SemaphoreType.DMA((copies,))] if copies else []),
        input_output_aliases=aliases or {},
        compiler_params=pltpu.CompilerParams(vmem_limit_bytes=mib * MIB),
        cost_estimate=pl.CostEstimate(flops=weight * US, bytes_accessed=1000, transcendentals=0),
        name=name,
    )(*[value for value, _ in ins])


def rows_at(block, size):
    return pl.ds(pl.multiple_of(block * size, size), size)


CORE, SHARD, CHIP_BIT_0, CHIP_BIT_1, KEEP_A, SEND_A, KEEP_B, SEND_B, CHIP = range(9)


def here(entry):
    shard, rep = lax.axis_index("fsdp"), lax.axis_index("rep")
    bit_a, bit_b = rep & 1, (rep >> 1) & 1
    table = (
        shard & 1, shard, (shard >> 1) & 1, (shard >> 2) & 1,
        bit_a, 1 - bit_a, 2 + bit_b, 3 - bit_b, shard >> 1,
    )
    return table[entry]


def reversed_bits(value, bits):
    return sum(((value >> bit) & 1) << (bits - 1 - bit) for bit in range(bits))


def open_kernel(
    scale, rate, x_ref, t_ref, w_ref, rep_ref, gram_keep, gram_send, x_out, w_out, first_a, first_b, keep_ref, *refs
):
    sends, (acc_ref, t_held, sems) = refs[:-3], refs[-3:]
    steps = keep_ref.shape[0]
    each_send = steps // len(sends)
    bits = steps.bit_length() - 1
    quarter = first_a.shape[0]
    depth = w_ref.shape[0]
    cut = depth // CUTS
    core = here(CORE)
    copy_x = pltpu.make_async_copy(x_ref, x_out, sems.at[0])
    copies_w = [
        pltpu.make_async_copy(w_ref.at[pl.ds(k * cut, cut)], w_out.at[pl.ds(k * cut, cut)], sems.at[4 + k])
        for k in range(CUTS)
    ]
    others = [
        pltpu.make_async_copy(t_ref, t_held, sems.at[1]),
        pltpu.make_async_copy(rep_ref.at[rows_at(here(SEND_A), quarter)], first_a, sems.at[2]),
        pltpu.make_async_copy(rep_ref.at[rows_at(here(SEND_B), quarter)], first_b, sems.at[3]),
    ]
    copy_x.start()
    copies_w[0].start()
    copies_w[1].start()
    copy_x.wait()
    x = x_out[...]
    gram = lax.dot_general(x, x, (((1,), (1,)), ((), ())), preferred_element_type=F32) * (rate * scale * scale)
    tiles = x.shape[0] // LANES
    pairs = [(i, j) for i in range(tiles) for j in range(i, tiles)]
    each = len(pairs) // 2
    for place, (i, j) in enumerate(pairs):
        part = gram[i * LANES : (i + 1) * LANES, j * LANES : (j + 1) * LANES].astype(BF16)
        side, spot = place // each, place % each
        rows = pl.ds(spot * LANES, LANES)

        @pl.when(core == side)
        def _():
            gram_keep[rows, :] = part

        @pl.when(core != side)
        def _():
            gram_send[rows, :] = part

    for k in range(CUTS):
        copies_w[k].wait()
        if k + 2 < CUTS:
            copies_w[k + 2].start()
        elif k + 2 == CUTS:
            for copy in others:
                copy.start()
        rows = pl.ds(k * cut, cut)
        part = jnp.dot(x_out[:, rows], w_out[rows, :].astype(BF16), preferred_element_type=F32)
        acc_ref[...] = part if k == 0 else acc_ref[...] + part
    others[0].wait()
    own = t_held.shape[0]
    rows = rows_at(here(SHARD), own)
    acc_ref[rows, :] = acc_ref[rows, :] - t_held[...].astype(F32) * (1.0 / scale)
    for j in range(steps):
        low = reversed_bits(j, bits) * SPAN
        for side in range(2):
            columns = slice(low + side * LANES, low + (side + 1) * LANES)

            @pl.when(core == side)
            def _():
                keep_ref[j] = (acc_ref[:, columns] * scale).astype(BF16)

            @pl.when(core != side)
            def _():
                sends[j // each_send][j % each_send] = (acc_ref[:, columns] * scale).astype(BF16)

    for copy in others[1:]:
        copy.wait()


CUTS = 4
SENDS = 2


def opening(x, t, w, rep_rows, scale, rate):
    tokens, depth = x.shape
    tiles = tokens // LANES
    each = tiles * (tiles + 1) // 4 * LANES
    quarter = (rep_rows.shape[0] // 4, rep_rows.shape[1])
    steps = w.shape[1] // SPAN
    return run(
        functools.partial(open_kernel, scale, rate),
        [near((each, LANES), BF16)] * 2
        + [near(x.shape, BF16), near(w.shape, F32)]
        + [near(quarter, BF16)] * 2
        + [near((steps, tokens, LANES), BF16)]
        + [near((steps // SENDS, tokens, LANES), BF16)] * SENDS,
        [(in_hbm(value), HBM) for value in (x, t, w, rep_rows)],
        4 + CUTS,
        scratch=[pltpu.VMEM((tokens, w.shape[1]), F32), pltpu.VMEM(t.shape, BF16)],
        weight=WEIGHT["opening"],
        name="opening",
    )


def fetch_kernel(token_ref, rep_ref, outer_ref, rep_a, rep_b, outer_a, outer_b, sems):
    del token_ref
    quarter = rep_a.shape[0]
    copies = []
    for k, (source, entry, target) in enumerate(
        [(rep_ref, KEEP_A, rep_a), (rep_ref, KEEP_B, rep_b), (outer_ref, KEEP_A, outer_a), (outer_ref, KEEP_B, outer_b)]
    ):
        copy = pltpu.make_async_copy(source.at[rows_at(here(entry), quarter)], target, sems.at[k])
        copy.start()
        copies.append(copy)
    for copy in copies:
        copy.wait()


def fetch(token, rep_rows, outer):
    quarter = (rep_rows.shape[0] // 4, rep_rows.shape[1])
    return run(
        fetch_kernel,
        [near(quarter, BF16)] * 2 + [near(quarter, F32)] * 2,
        [(token, HBM), (in_hbm(rep_rows), HBM), (in_hbm(outer), HBM)],
        4,
        weight=WEIGHT["fetch"],
        name="fetch",
    )


def fold_kernel(entry, token_ref, own_ref, *refs):
    gots, leave_ref, stay_ref = refs[:-2], refs[-2], refs[-1]
    size = stay_ref.shape[0]
    each = own_ref.shape[0] // len(gots)

    def total(place):
        got = gots[place // each]
        got = got[...] if each == 1 and len(got.shape) == 2 else got[place % each]
        return own_ref[place].astype(F32) + got.astype(F32)

    for side in range(2):

        @pl.when(here(entry) == side)
        def _():
            for k in range(size):
                leave_ref[k] = total((1 - side) * size + k).astype(BF16)
                stay_ref[k] = total(side * size + k)


def fold(token, own, gots, entry, weight):
    size, tokens, width = own.shape
    shape = (size // 2, tokens, width)
    return run(
        functools.partial(fold_kernel, entry),
        [near(shape, BF16), near(shape, F32)],
        [(token, HBM), (own, VMEM)] + [(got, VMEM) for got in gots],
        0,
        weight=weight,
        name="fold",
    )


def add_kernel(own_ref, got_ref, out_ref):
    out_ref[...] = (own_ref[...].astype(F32) + got_ref[...].astype(F32)).astype(BF16)


def add(own, got, weight):
    return run(
        add_kernel,
        [near(own.shape, BF16)],
        [(own, VMEM), (got, VMEM)],
        0,
        weight=weight,
        name="add",
    )[0]


def whole_gram_kernel(token_ref, x_ref, near_ref, far_ref, other_near, other_far, out_ref, turned_ref, pack_ref):
    rows = near_ref.shape[0]
    core, side = here(CORE), here(CHIP_BIT_0)
    for ref, half, part in (
        (near_ref, core, side),
        (far_ref, core, 1 - side),
        (other_near, 1 - core, side),
        (other_far, 1 - core, 1 - side),
    ):
        pack_ref[rows_at(2 * half + part, rows), :] = ref[...]
    tiles = out_ref.shape[0] // LANES
    pairs = [(i, j) for i in range(tiles) for j in range(i, tiles)]
    for place, (i, j) in enumerate(pairs):
        part = pack_ref[place * LANES : (place + 1) * LANES, :]
        out_ref[i * LANES : (i + 1) * LANES, j * LANES : (j + 1) * LANES] = part
        if i != j:
            out_ref[j * LANES : (j + 1) * LANES, i * LANES : (i + 1) * LANES] = part.T
    turned_ref[...] = x_ref[...].T


def whole_gram(token, x, pieces):
    tokens, depth = x.shape
    return run(
        whole_gram_kernel,
        [near((tokens, tokens), BF16), near((depth, tokens), BF16)],
        [(token, HBM), (x, VMEM)] + [(piece, VMEM) for piece in pieces],
        0,
        scratch=[pltpu.VMEM((4 * pieces[0].shape[0], LANES), BF16)],
        weight=WEIGHT["whole_gram"],
        name="whole_gram",
    )


def residual_kernel(own_ref, got_ref, gram_ref, out_ref):
    error = own_ref[0] + got_ref[0].astype(F32)
    moved = jnp.dot(gram_ref[...], error.astype(BF16), preferred_element_type=F32)
    out_ref[...] = (2.0 * error - moved).astype(BF16)


def residual(own, got, gram):
    _, tokens, width = own.shape
    return run(
        residual_kernel,
        [near((tokens, width), BF16)],
        [(own, VMEM), (got, VMEM), (gram, VMEM)],
        0,
        weight=WEIGHT["residual"],
        name="residual",
    )[0]


def step_kernel(rate, places, token_ref, turned_ref, w_ref, *refs):
    count = len(places)
    pieces = refs[: 2 * count]
    out_ref, pair_ref, buffer_ref, sems = refs[-4:]
    first = here(CORE) == 0
    copies = []
    for k, flip in enumerate(places):
        mine, other = pieces[2 * k][...], pieces[2 * k + 1][...]
        pair_ref[:, :LANES] = jnp.where(first, mine, other)
        pair_ref[:, LANES:] = jnp.where(first, other, mine)
        place = jnp.bitwise_xor(here(CHIP), flip)
        grad = jnp.dot(turned_ref[...], pair_ref[...], preferred_element_type=F32)
        columns = pl.ds(pl.multiple_of(place * SPAN, SPAN), SPAN)
        buffer_ref[k] = w_ref[:, columns] - rate * grad
        copy = pltpu.make_async_copy(
            buffer_ref.at[k], out_ref.at[:, columns], sems.at[k]
        )
        copy.start()
        copies.append(copy)
    for copy in copies:
        copy.wait()


def weight_step(token, turned, w, pairs, places, rate, before):
    depth, tokens = turned.shape
    count = len(pairs)
    flat = [piece for pair in pairs for piece in pair]
    ins = [(token, HBM), (turned, VMEM), (w, VMEM)] + [(piece, VMEM) for piece in flat]
    aliases = {}
    if before is not None:
        aliases = {len(ins): 0}
        ins.append((before, HBM))
    return run(
        functools.partial(step_kernel, rate, tuple(places)),
        [far(w.shape, F32)],
        ins,
        count,
        scratch=[pltpu.VMEM((tokens, SPAN), BF16), pltpu.VMEM((count, depth, SPAN), F32)],
        aliases=aliases,
        weight=WEIGHT["weight_step"],
        name="weight_step",
    )[0]


def first_code_kernel(rep_ref, got_ref, outer_ref, code_ref):
    total = rep_ref[...].astype(F32) + got_ref[...].astype(F32)
    code_ref[...] = encode(total, outer_ref[...], 2.0)


def second_code_kernel(own_ref, got_ref, outer_ref, code_ref):
    outer = outer_ref[...]
    total = decode_total(own_ref[...], outer, 2.0) + decode_total(got_ref[...], outer, 2.0)
    code_ref[...] = encode(total, outer, 4.0)


def code(kernel, own, got, outer_rows, weight):
    return run(
        kernel,
        [near(own.shape, BF16)],
        [(own, VMEM), (got, VMEM), (outer_rows, VMEM)],
        0,
        weight=weight,
        name="code",
    )[0]


PART = 128


def update_rows(entries, codes, outers, moments, reps, outs, buffers, sems, ready):
    size = codes[0].shape[0]
    copies = []
    part = min(PART, size)
    for half in range(2):
        for cut in range(size // part):
            spot = half * (size // part) + cut
            rows = pl.ds(cut * part, part)
            held = pl.ds(spot * part, part)
            if cut == 0:
                ready(half)
            outer = outers[half][rows, :]
            delta = decode_away(codes[half][rows, :], outer, 4.0) * 0.25
            moment = momentum_coef * moments[half][rows, :] + delta
            new_outer = outer - outer_rate * (delta + momentum_coef * moment)
            mixed = merge_keep * reps[half][rows, :].astype(F32) + (1.0 - merge_keep) * new_outer
            for k, value in enumerate((new_outer, moment, mixed.astype(BF16))):
                buffers[k][held, :] = value
                target = rows_at(here(entries[half]) * (size // part) + cut, part)
                copy = pltpu.make_async_copy(buffers[k].at[held], outs[k].at[target], sems.at[3 * spot + k])
                copy.start()
                copies.append(copy)
    for copy in copies:
        copy.wait()


def near_update_kernel(
    token_ref, code_a, code_b, outer_a, outer_b, rep_a, rep_b, outer_ref, moment_ref, rep_ref,
    new_outer, new_moment, merged, far_outer_a, far_outer_b, far_moment_a, far_moment_b, far_rep_a, far_rep_b,
    moment_a, moment_b, buffer_outer, buffer_moment, buffer_merged, sems,
):
    size = code_a.shape[0]
    base = 6 * max(size // PART, 1)
    fetches = [
        (moment_ref, KEEP_A, moment_a),
        (moment_ref, KEEP_B, moment_b),
        (outer_ref, SEND_A, far_outer_a),
        (outer_ref, SEND_B, far_outer_b),
        (moment_ref, SEND_A, far_moment_a),
        (moment_ref, SEND_B, far_moment_b),
        (rep_ref, SEND_A, far_rep_a),
        (rep_ref, SEND_B, far_rep_b),
    ]
    copies = []
    for k, (source, entry, target) in enumerate(fetches):
        copy = pltpu.make_async_copy(source.at[rows_at(here(entry), size)], target, sems.at[base + k])
        copy.start()
        copies.append(copy)
    update_rows(
        (KEEP_A, KEEP_B), (code_a, code_b), (outer_a, outer_b), (moment_a, moment_b), (rep_a, rep_b),
        (new_outer, new_moment, merged), (buffer_outer, buffer_moment, buffer_merged), sems,
        lambda half: copies[half].wait(),
    )
    for copy in copies[2:]:
        copy.wait()


def far_update_kernel(
    token_ref, code_a, code_b, outer_a, outer_b, moment_a, moment_b, rep_a, rep_b, held_a, held_b, held_c,
    new_outer, new_moment, merged, buffer_outer, buffer_moment, buffer_merged, sems,
):
    del held_a, held_b, held_c
    update_rows(
        (SEND_A, SEND_B), (code_a, code_b), (outer_a, outer_b), (moment_a, moment_b), (rep_a, rep_b),
        (new_outer, new_moment, merged), (buffer_outer, buffer_moment, buffer_merged), sems,
        lambda half: None,
    )


def update_scratch(size, width):
    return [pltpu.VMEM((2 * size, width), dtype) for dtype in (F32, F32, BF16)]


def near_update(token, codes, outers, reps, outer, moment, rep_rows):
    size, width = codes[0].shape
    full = outer.shape
    return run(
        near_update_kernel,
        [far(full, F32), far(full, F32), far(full, BF16)]
        + [near((size, width), F32)] * 4
        + [near((size, width), BF16)] * 2,
        [(token, HBM)]
        + [(value, VMEM) for value in (*codes, *outers, *reps)]
        + [(in_hbm(value), HBM) for value in (outer, moment, rep_rows)],
        6 * max(size // PART, 1) + 8,
        scratch=[pltpu.VMEM((size, width), F32)] * 2 + update_scratch(size, width),
        mib=16,
        weight=WEIGHT["near_update"],
        name="near_update",
    )


def far_update(token, codes, fetched, before):
    size, width = codes[0].shape
    outs = [far(value.shape, value.dtype) for value in before]
    ins = [(token, HBM)] + [(value, VMEM) for value in (*codes, *fetched)]
    return run(
        far_update_kernel,
        outs,
        ins + [(value, HBM) for value in before],
        6 * max(size // PART, 1),
        scratch=update_scratch(size, width),
        mib=16,
        aliases={len(ins) + k: k for k in range(3)},
        weight=WEIGHT["far_update"],
        name="far_update",
    )


def after(value, *others):
    return lax.optimization_barrier((value, *others))[0]


def both(x, t, w, outer, moment, rep_rows):
    shards = lax.axis_size("fsdp")
    chips = shards // 2
    scale = (x.shape[1] * shards) ** -0.5
    rate = inner_rate * scale
    token = t

    gram_keep, gram_send, x, w, first_a, first_b, keep, *sends = opening(x, t, w, rep_rows, scale, inner_rate)
    gram_got = swap(gram_send, "fsdp", 1)
    got = [swap(send, "fsdp", 1) for send in sends]
    got_a, got_b = swap(first_a, "rep", 1), swap(first_b, "rep", 2)
    halves = (2, gram_keep.shape[0] // 2, LANES)
    gram_leave, gram_stay = fold(
        token, gram_keep.reshape(halves), [gram_got.reshape(halves)], CHIP_BIT_0, WEIGHT["add_1"]
    )
    gram_got = swap(gram_leave[0], "fsdp", 2)

    leave_1, stay = fold(after(token, gram_leave), keep, got, CHIP_BIT_0, WEIGHT["fold_1"])
    got = swap(leave_1, "fsdp", 2)
    rep_a, rep_b, outer_a, outer_b = fetch(after(token, leave_1), rep_rows, outer)
    gram_2 = add(after(gram_stay, rep_a)[0], gram_got, WEIGHT["add_2"])
    gram_got = swap(gram_2, "fsdp", 4)

    leave_2, stay = fold(token, after(stay, gram_2), [got], CHIP_BIT_1, WEIGHT["fold_2"])
    got = swap(leave_2, "fsdp", 4)
    code_a = code(first_code_kernel, after(rep_a, leave_2), got_a, outer_a, WEIGHT["code_1"])
    code_b = code(first_code_kernel, after(rep_b, code_a), got_b, outer_b, WEIGHT["code_2"])
    got_a = swap(code_a, "rep", 2)
    got_b = swap(code_b, "rep", 1)

    gram_3 = add(after(gram_2, leave_2, code_a), gram_got, WEIGHT["add_3"])
    gram_far = swap(gram_3, "fsdp", 2)
    pieces = [gram_3, gram_far]
    pieces += [swap(piece, "fsdp", 1) for piece in pieces]

    gram, turned = whole_gram(after(token, leave_2), x, pieces)
    moved = residual(stay, got, gram)
    code_a = code(second_code_kernel, after(code_a, moved), got_a, outer_a, WEIGHT["code_3"])
    code_b = code(second_code_kernel, after(code_b, code_a), got_b, outer_b, WEIGHT["code_4"])
    got_a = swap(code_a, "rep", 1)
    got_b = swap(code_b, "rep", 2)

    updated = near_update(
        after(token, moved), (code_a, code_b), (outer_a, outer_b), (rep_a, rep_b), outer, moment, rep_rows
    )
    mine = [moved] + [swap(moved, "fsdp", 2 * k) for k in range(1, chips)]
    mine = [after(piece, updated[0]) for piece in mine]
    pairs = [(piece, swap(piece, "fsdp", 1)) for piece in mine]
    result = weight_step(token, turned, w, pairs, range(chips), rate, None)
    outers = far_update(after(token, result), (got_a, got_b), updated[3:], updated[:3])
    return result, *outers


def plain_outer(outer, moment, rep_rows):
    replica_rows = rep_rows.astype(F32)
    delta = lax.psum(outer - replica_rows, "rep") / lax.axis_size("rep")
    new_moment = momentum_coef * moment + delta
    new_outer = outer - outer_rate * (delta + momentum_coef * new_moment)
    mixed = merge_keep * replica_rows + (1.0 - merge_keep) * new_outer
    return new_outer, new_moment, mixed.astype(BF16)


def plain_inner(x, t, w):
    scale = (x.shape[1] * lax.axis_size("fsdp")) ** -0.5
    for _ in range(INNER):
        part = jnp.dot(x, w.astype(BF16), preferred_element_type=F32).astype(BF16)
        predicted = lax.psum_scatter(part, "fsdp", scatter_dimension=0, tiled=True).astype(F32) * scale
        errors = lax.all_gather((predicted - t.astype(F32)).astype(BF16), "fsdp", axis=0, tiled=True)
        gradient = lax.dot_general(x, errors, (((0,), (0,)), ((), ())), preferred_element_type=F32)
        w = w - inner_rate * scale * gradient
    return w


def local(tokens, targets, inner_weights, outer_weights, outer_momentum, replica_weights):
    x, t, w, rep_rows = tokens[0], targets[0], inner_weights[0], replica_weights[0]
    tiles = x.shape[0] // LANES
    if (
        lax.axis_size("fsdp") == 8
        and lax.axis_size("rep") == 4
        and w.shape[1] == 8 * LANES
        and x.shape[0] % LANES == 0
        and tiles * (tiles + 1) % 4 == 0
        and rep_rows.shape[0] % (4 * PART) == 0
    ):
        new_inner, new_outer, new_moment, merged = both(x, t, w, outer_weights, outer_momentum, rep_rows)
    else:
        new_outer, new_moment, merged = plain_outer(outer_weights, outer_momentum, rep_rows)
        new_inner = plain_inner(x, t, w)
    return new_inner[None], new_outer, new_moment, merged[None]


def solution(mesh):
    placed = (
        P("rep", None, "fsdp"),
        P("rep", "fsdp", None),
        P("rep", "fsdp", None),
        P("fsdp", None),
        P("fsdp", None),
        P("rep", "fsdp", None),
    )
    return jax.shard_map(
        local,
        mesh=mesh,
        in_specs=placed,
        out_specs=(
            P("rep", "fsdp", None),
            P("fsdp", None),
            P("fsdp", None),
            P("rep", "fsdp", None),
        ),
        check_vma=False,
    )
```

```python
import functools

import jax
import jax.numpy as jnp
from jax import lax
from jax.experimental import pallas as pl
from jax.experimental.pallas import tpu as pltpu
from jax.sharding import PartitionSpec as P

INNER = 2

inner_rate = 0.5
momentum_coef = 0.9
outer_rate = 0.7
merge_keep = 0.5

F32 = jnp.float32
BF16 = jnp.bfloat16
LANES = 128
SPAN = 2 * LANES
MIB = 1 << 20
US = 1150000000

CODE_SCALE = 2.0**60
CODE_LEAST = 2.0**-30
CODE_CUT = 2.0**20


WEIGHT = {
    "prefetch": 0,
    "opening": 1,
    "fetch": 0,
    "add_1": 0,
    "add_2": 20,
    "add_3": 20,
    "fold_1": 20,
    "fold_2": 8,
    "code_1": 0,
    "code_2": 0,
    "code_3": 0,
    "code_4": 0,
    "whole_gram": 0,
    "residual": 4,
    "near_update": 20,
    "weight_step": 0,
    "far_update": 0,
}


def encode(total, outer_rows, count):
    away = count * outer_rows - total
    held = jnp.where(jnp.abs(total) < CODE_LEAST, CODE_LEAST, total) * CODE_SCALE
    return jnp.where(jnp.abs(total) < jnp.abs(away), held, away).astype(BF16)


def decode_total(code, outer_rows, count):
    code = code.astype(F32)
    return jnp.where(jnp.abs(code) > CODE_CUT, code * (1.0 / CODE_SCALE), count * outer_rows - code)


def decode_away(code, outer_rows, count):
    code = code.astype(F32)
    return jnp.where(jnp.abs(code) > CODE_CUT, count * outer_rows - code * (1.0 / CODE_SCALE), code)


def swap(value, axis, flip):
    count = lax.axis_size(axis)
    return lax.ppermute(value, axis, [(i, i ^ flip) for i in range(count)])


VMEM = pl.BlockSpec(memory_space=pltpu.VMEM)
HBM = pl.BlockSpec(memory_space=pl.ANY)
SMEM = pl.BlockSpec(memory_space=pltpu.SMEM)


def in_hbm(value):
    return pltpu.with_memory_space_constraint(value, pltpu.HBM)


def near(shape, dtype):
    return pltpu.VMEM(tuple(shape), dtype)


def far(shape, dtype):
    return pltpu.HBM(tuple(shape), dtype)


def run(kernel, outs, ins, copies, scratch=(), weight=0, mib=8, aliases=None, name="kernel"):
    specs = [spec for _, spec in ins]
    return pl.pallas_call(
        kernel,
        out_shape=tuple(outs),
        in_specs=specs,
        out_specs=tuple(VMEM if out.memory_space == pltpu.VMEM else HBM for out in outs),
        scratch_shapes=list(scratch) + ([pltpu.SemaphoreType.DMA((copies,))] if copies else []),
        input_output_aliases=aliases or {},
        compiler_params=pltpu.CompilerParams(vmem_limit_bytes=mib * MIB),
        cost_estimate=pl.CostEstimate(flops=weight * US, bytes_accessed=1000, transcendentals=0),
        name=name,
    )(*[value for value, _ in ins])


def rows_at(block, size):
    return pl.ds(pl.multiple_of(block * size, size), size)


CORE, SHARD, CHIP_BIT_0, CHIP_BIT_1, KEEP_A, SEND_A, KEEP_B, SEND_B, CHIP = range(9)


def here(entry):
    shard, rep = lax.axis_index("fsdp"), lax.axis_index("rep")
    bit_a, bit_b = rep & 1, (rep >> 1) & 1
    table = (
        shard & 1, shard, (shard >> 1) & 1, (shard >> 2) & 1,
        bit_a, 1 - bit_a, 2 + bit_b, 3 - bit_b, shard >> 1,
    )
    return table[entry]


def reversed_bits(value, bits):
    return sum(((value >> bit) & 1) << (bits - 1 - bit) for bit in range(bits))


def open_kernel(
    scale, rate, x_ref, t_ref, w_ref, rep_ref, gram_keep, gram_send, x_out, w_out, first_a, first_b, keep_ref, *refs
):
    sends, (acc_ref, t_held, sems) = refs[:-3], refs[-3:]
    steps = keep_ref.shape[0]
    each_send = steps // len(sends)
    bits = steps.bit_length() - 1
    quarter = first_a.shape[0]
    depth = w_ref.shape[0]
    cut = depth // CUTS
    core = here(CORE)
    copy_x = pltpu.make_async_copy(x_ref, x_out, sems.at[0])
    copies_w = [
        pltpu.make_async_copy(w_ref.at[pl.ds(k * cut, cut)], w_out.at[pl.ds(k * cut, cut)], sems.at[4 + k])
        for k in range(CUTS)
    ]
    others = [
        pltpu.make_async_copy(t_ref, t_held, sems.at[1]),
        pltpu.make_async_copy(rep_ref.at[rows_at(here(SEND_A), quarter)], first_a, sems.at[2]),
        pltpu.make_async_copy(rep_ref.at[rows_at(here(SEND_B), quarter)], first_b, sems.at[3]),
    ]
    for copy in (copy_x, *copies_w, *others):
        copy.start()
    copy_x.wait()
    x = x_out[...]
    gram = lax.dot_general(x, x, (((1,), (1,)), ((), ())), preferred_element_type=F32) * (rate * scale * scale)
    tiles = x.shape[0] // LANES
    pairs = [(i, j) for i in range(tiles) for j in range(i, tiles)]
    each = len(pairs) // 2
    for place, (i, j) in enumerate(pairs):
        part = gram[i * LANES : (i + 1) * LANES, j * LANES : (j + 1) * LANES].astype(BF16)
        side, spot = place // each, place % each
        rows = pl.ds(spot * LANES, LANES)

        @pl.when(core == side)
        def _():
            gram_keep[rows, :] = part

        @pl.when(core != side)
        def _():
            gram_send[rows, :] = part

    for k in range(CUTS):
        copies_w[k].wait()
        rows = pl.ds(k * cut, cut)
        part = jnp.dot(x_out[:, rows], w_out[rows, :].astype(BF16), preferred_element_type=F32)
        acc_ref[...] = part if k == 0 else acc_ref[...] + part
    others[0].wait()
    own = t_held.shape[0]
    rows = rows_at(here(SHARD), own)
    acc_ref[rows, :] = acc_ref[rows, :] - t_held[...].astype(F32) * (1.0 / scale)
    for j in range(steps):
        low = reversed_bits(j, bits) * SPAN
        for side in range(2):
            columns = slice(low + side * LANES, low + (side + 1) * LANES)

            @pl.when(core == side)
            def _():
                keep_ref[j] = (acc_ref[:, columns] * scale).astype(BF16)

            @pl.when(core != side)
            def _():
                sends[j // each_send][j % each_send] = (acc_ref[:, columns] * scale).astype(BF16)

    for copy in others[1:]:
        copy.wait()


CUTS = 4
SENDS = 2


def opening(x, t, w, rep_rows, scale, rate):
    tokens, depth = x.shape
    tiles = tokens // LANES
    each = tiles * (tiles + 1) // 4 * LANES
    quarter = (rep_rows.shape[0] // 4, rep_rows.shape[1])
    steps = w.shape[1] // SPAN
    return run(
        functools.partial(open_kernel, scale, rate),
        [near((each, LANES), BF16)] * 2
        + [near(x.shape, BF16), near(w.shape, F32)]
        + [near(quarter, BF16)] * 2
        + [near((steps, tokens, LANES), BF16)]
        + [near((steps // SENDS, tokens, LANES), BF16)] * SENDS,
        [(in_hbm(value), HBM) for value in (x, t, w, rep_rows)],
        4 + CUTS,
        scratch=[pltpu.VMEM((tokens, w.shape[1]), F32), pltpu.VMEM(t.shape, BF16)],
        weight=WEIGHT["opening"],
        name="opening",
    )


def prefetch_kernel(
    token_ref, outer_ref, moment_ref, rep_ref,
    moment_a, moment_b, far_outer_a, far_outer_b, far_moment_a, far_moment_b, far_rep_a, far_rep_b, sems,
):
    del token_ref
    quarter = moment_a.shape[0]
    copies = []
    for k, (source, entry, target) in enumerate(
        [
            (moment_ref, KEEP_A, moment_a),
            (moment_ref, KEEP_B, moment_b),
            (outer_ref, SEND_A, far_outer_a),
            (outer_ref, SEND_B, far_outer_b),
            (moment_ref, SEND_A, far_moment_a),
            (moment_ref, SEND_B, far_moment_b),
            (rep_ref, SEND_A, far_rep_a),
            (rep_ref, SEND_B, far_rep_b),
        ]
    ):
        copy = pltpu.make_async_copy(source.at[rows_at(here(entry), quarter)], target, sems.at[k])
        copy.start()
        copies.append(copy)
    for copy in copies:
        copy.wait()


def prefetch(token, outer, moment, rep_rows):
    quarter = (outer.shape[0] // 4, outer.shape[1])
    return run(
        prefetch_kernel,
        [near(quarter, F32)] * 6 + [near(quarter, BF16)] * 2,
        [(token, HBM)] + [(in_hbm(value), HBM) for value in (outer, moment, rep_rows)],
        8,
        weight=WEIGHT["prefetch"],
        name="prefetch",
    )


def fetch_kernel(token_ref, rep_ref, outer_ref, rep_a, rep_b, outer_a, outer_b, sems):
    del token_ref
    quarter = rep_a.shape[0]
    copies = []
    for k, (source, entry, target) in enumerate(
        [(rep_ref, KEEP_A, rep_a), (rep_ref, KEEP_B, rep_b), (outer_ref, KEEP_A, outer_a), (outer_ref, KEEP_B, outer_b)]
    ):
        copy = pltpu.make_async_copy(source.at[rows_at(here(entry), quarter)], target, sems.at[k])
        copy.start()
        copies.append(copy)
    for copy in copies:
        copy.wait()


def fetch(token, rep_rows, outer):
    quarter = (rep_rows.shape[0] // 4, rep_rows.shape[1])
    return run(
        fetch_kernel,
        [near(quarter, BF16)] * 2 + [near(quarter, F32)] * 2,
        [(token, HBM), (in_hbm(rep_rows), HBM), (in_hbm(outer), HBM)],
        4,
        weight=WEIGHT["fetch"],
        name="fetch",
    )


def fold_kernel(entry, token_ref, own_ref, *refs):
    gots, leave_ref, stay_ref = refs[:-2], refs[-2], refs[-1]
    size = stay_ref.shape[0]
    each = own_ref.shape[0] // len(gots)

    def total(place):
        got = gots[place // each]
        got = got[...] if each == 1 and len(got.shape) == 2 else got[place % each]
        return own_ref[place].astype(F32) + got.astype(F32)

    for side in range(2):

        @pl.when(here(entry) == side)
        def _():
            for k in range(size):
                leave_ref[k] = total((1 - side) * size + k).astype(BF16)
                stay_ref[k] = total(side * size + k)


def fold(token, own, gots, entry, weight):
    size, tokens, width = own.shape
    shape = (size // 2, tokens, width)
    return run(
        functools.partial(fold_kernel, entry),
        [near(shape, BF16), near(shape, F32)],
        [(token, HBM), (own, VMEM)] + [(got, VMEM) for got in gots],
        0,
        weight=weight,
        name="fold",
    )


def add_kernel(own_ref, got_ref, out_ref):
    out_ref[...] = (own_ref[...].astype(F32) + got_ref[...].astype(F32)).astype(BF16)


def add(own, got, weight):
    return run(
        add_kernel,
        [near(own.shape, BF16)],
        [(own, VMEM), (got, VMEM)],
        0,
        weight=weight,
        name="add",
    )[0]


def whole_gram_kernel(token_ref, x_ref, near_ref, far_ref, other_near, other_far, out_ref, turned_ref, pack_ref):
    rows = near_ref.shape[0]
    core, side = here(CORE), here(CHIP_BIT_0)
    for ref, half, part in (
        (near_ref, core, side),
        (far_ref, core, 1 - side),
        (other_near, 1 - core, side),
        (other_far, 1 - core, 1 - side),
    ):
        pack_ref[rows_at(2 * half + part, rows), :] = ref[...]
    tiles = out_ref.shape[0] // LANES
    pairs = [(i, j) for i in range(tiles) for j in range(i, tiles)]
    for place, (i, j) in enumerate(pairs):
        part = pack_ref[place * LANES : (place + 1) * LANES, :]
        out_ref[i * LANES : (i + 1) * LANES, j * LANES : (j + 1) * LANES] = part
        if i != j:
            out_ref[j * LANES : (j + 1) * LANES, i * LANES : (i + 1) * LANES] = part.T
    turned_ref[...] = x_ref[...].T


def whole_gram(token, x, pieces):
    tokens, depth = x.shape
    return run(
        whole_gram_kernel,
        [near((tokens, tokens), BF16), near((depth, tokens), BF16)],
        [(token, HBM), (x, VMEM)] + [(piece, VMEM) for piece in pieces],
        0,
        scratch=[pltpu.VMEM((4 * pieces[0].shape[0], LANES), BF16)],
        weight=WEIGHT["whole_gram"],
        name="whole_gram",
    )


def residual_kernel(own_ref, got_ref, gram_ref, out_ref):
    error = own_ref[0] + got_ref[0].astype(F32)
    moved = jnp.dot(gram_ref[...], error.astype(BF16), preferred_element_type=F32)
    out_ref[...] = (2.0 * error - moved).astype(BF16)


def residual(own, got, gram):
    _, tokens, width = own.shape
    return run(
        residual_kernel,
        [near((tokens, width), BF16)],
        [(own, VMEM), (got, VMEM), (gram, VMEM)],
        0,
        weight=WEIGHT["residual"],
        name="residual",
    )[0]


def step_kernel(rate, places, token_ref, turned_ref, w_ref, *refs):
    count = len(places)
    pieces = refs[: 2 * count]
    out_ref, pair_ref, buffer_ref, sems = refs[-4:]
    first = here(CORE) == 0
    copies = []
    for k, flip in enumerate(places):
        mine, other = pieces[2 * k][...], pieces[2 * k + 1][...]
        pair_ref[:, :LANES] = jnp.where(first, mine, other)
        pair_ref[:, LANES:] = jnp.where(first, other, mine)
        place = jnp.bitwise_xor(here(CHIP), flip)
        grad = jnp.dot(turned_ref[...], pair_ref[...], preferred_element_type=F32)
        columns = pl.ds(pl.multiple_of(place * SPAN, SPAN), SPAN)
        buffer_ref[k] = w_ref[:, columns] - rate * grad
        copy = pltpu.make_async_copy(
            buffer_ref.at[k], out_ref.at[:, columns], sems.at[k]
        )
        copy.start()
        copies.append(copy)
    for copy in copies:
        copy.wait()


def weight_step(token, turned, w, pairs, places, rate, before):
    depth, tokens = turned.shape
    count = len(pairs)
    flat = [piece for pair in pairs for piece in pair]
    ins = [(token, HBM), (turned, VMEM), (w, VMEM)] + [(piece, VMEM) for piece in flat]
    aliases = {}
    if before is not None:
        aliases = {len(ins): 0}
        ins.append((before, HBM))
    return run(
        functools.partial(step_kernel, rate, tuple(places)),
        [far(w.shape, F32)],
        ins,
        count,
        scratch=[pltpu.VMEM((tokens, SPAN), BF16), pltpu.VMEM((count, depth, SPAN), F32)],
        aliases=aliases,
        weight=WEIGHT["weight_step"],
        name="weight_step",
    )[0]


def first_code_kernel(rep_ref, got_ref, outer_ref, code_ref):
    total = rep_ref[...].astype(F32) + got_ref[...].astype(F32)
    code_ref[...] = encode(total, outer_ref[...], 2.0)


def second_code_kernel(own_ref, got_ref, outer_ref, code_ref):
    outer = outer_ref[...]
    total = decode_total(own_ref[...], outer, 2.0) + decode_total(got_ref[...], outer, 2.0)
    code_ref[...] = encode(total, outer, 4.0)


def code(kernel, own, got, outer_rows, weight):
    return run(
        kernel,
        [near(own.shape, BF16)],
        [(own, VMEM), (got, VMEM), (outer_rows, VMEM)],
        0,
        weight=weight,
        name="code",
    )[0]


PART = 128


def update_rows(entries, codes, outers, moments, reps, outs, buffers, sems, ready):
    size = codes[0].shape[0]
    copies = []
    part = min(PART, size)
    for half in range(2):
        for cut in range(size // part):
            spot = half * (size // part) + cut
            rows = pl.ds(cut * part, part)
            held = pl.ds(spot * part, part)
            if cut == 0:
                ready(half)
            outer = outers[half][rows, :]
            delta = decode_away(codes[half][rows, :], outer, 4.0) * 0.25
            moment = momentum_coef * moments[half][rows, :] + delta
            new_outer = outer - outer_rate * (delta + momentum_coef * moment)
            mixed = merge_keep * reps[half][rows, :].astype(F32) + (1.0 - merge_keep) * new_outer
            for k, value in enumerate((new_outer, moment, mixed.astype(BF16))):
                buffers[k][held, :] = value
                target = rows_at(here(entries[half]) * (size // part) + cut, part)
                copy = pltpu.make_async_copy(buffers[k].at[held], outs[k].at[target], sems.at[3 * spot + k])
                copy.start()
                copies.append(copy)
    for copy in copies:
        copy.wait()


def near_update_kernel(
    token_ref, code_a, code_b, outer_a, outer_b, moment_a, moment_b, rep_a, rep_b,
    new_outer, new_moment, merged, buffer_outer, buffer_moment, buffer_merged, sems,
):
    del token_ref
    update_rows(
        (KEEP_A, KEEP_B), (code_a, code_b), (outer_a, outer_b), (moment_a, moment_b), (rep_a, rep_b),
        (new_outer, new_moment, merged), (buffer_outer, buffer_moment, buffer_merged), sems,
        lambda half: None,
    )


def far_update_kernel(
    token_ref, code_a, code_b, outer_a, outer_b, moment_a, moment_b, rep_a, rep_b, held_a, held_b, held_c,
    new_outer, new_moment, merged, buffer_outer, buffer_moment, buffer_merged, sems,
):
    del held_a, held_b, held_c
    update_rows(
        (SEND_A, SEND_B), (code_a, code_b), (outer_a, outer_b), (moment_a, moment_b), (rep_a, rep_b),
        (new_outer, new_moment, merged), (buffer_outer, buffer_moment, buffer_merged), sems,
        lambda half: None,
    )


def update_scratch(size, width):
    return [pltpu.VMEM((2 * size, width), dtype) for dtype in (F32, F32, BF16)]


def near_update(token, codes, outers, moments, reps, full):
    size, width = codes[0].shape
    return run(
        near_update_kernel,
        [far(full, F32), far(full, F32), far(full, BF16)],
        [(token, HBM)] + [(value, VMEM) for value in (*codes, *outers, *moments, *reps)],
        6 * max(size // PART, 1),
        scratch=update_scratch(size, width),
        mib=16,
        weight=WEIGHT["near_update"],
        name="near_update",
    )


def far_update(token, codes, fetched, before):
    size, width = codes[0].shape
    outs = [far(value.shape, value.dtype) for value in before]
    ins = [(token, HBM)] + [(value, VMEM) for value in (*codes, *fetched)]
    return run(
        far_update_kernel,
        outs,
        ins + [(value, HBM) for value in before],
        6 * max(size // PART, 1),
        scratch=update_scratch(size, width),
        mib=16,
        aliases={len(ins) + k: k for k in range(3)},
        weight=WEIGHT["far_update"],
        name="far_update",
    )


def after(value, *others):
    return lax.optimization_barrier((value, *others))[0]


def both(x, t, w, outer, moment, rep_rows):
    shards = lax.axis_size("fsdp")
    chips = shards // 2
    scale = (x.shape[1] * shards) ** -0.5
    rate = inner_rate * scale
    token = t

    gram_keep, gram_send, x, w, first_a, first_b, keep, *sends = opening(x, t, w, rep_rows, scale, inner_rate)
    gram_got = swap(gram_send, "fsdp", 1)
    got = [swap(send, "fsdp", 1) for send in sends]
    got_a, got_b = swap(first_a, "rep", 1), swap(first_b, "rep", 2)
    halves = (2, gram_keep.shape[0] // 2, LANES)
    gram_leave, gram_stay = fold(
        token, gram_keep.reshape(halves), [gram_got.reshape(halves)], CHIP_BIT_0, WEIGHT["add_1"]
    )
    gram_got = swap(gram_leave[0], "fsdp", 2)

    leave_1, stay = fold(after(token, gram_leave), keep, got, CHIP_BIT_0, WEIGHT["fold_1"])
    got = swap(leave_1, "fsdp", 2)
    rep_a, rep_b, outer_a, outer_b = fetch(after(token, leave_1), rep_rows, outer)
    gram_2 = add(after(gram_stay, rep_a)[0], gram_got, WEIGHT["add_2"])
    gram_got = swap(gram_2, "fsdp", 4)

    fetched = prefetch(after(token, gram_2), outer, moment, rep_rows)
    leave_2, stay = fold(token, after(stay, gram_2, fetched[0]), [got], CHIP_BIT_1, WEIGHT["fold_2"])
    got = swap(leave_2, "fsdp", 4)
    code_a = code(first_code_kernel, after(rep_a, leave_2), got_a, outer_a, WEIGHT["code_1"])
    code_b = code(first_code_kernel, after(rep_b, code_a), got_b, outer_b, WEIGHT["code_2"])
    got_a = swap(code_a, "rep", 2)
    got_b = swap(code_b, "rep", 1)

    gram_3 = add(after(gram_2, leave_2), gram_got, WEIGHT["add_3"])
    gram_far = swap(gram_3, "fsdp", 2)
    pieces = [gram_3, gram_far, swap(gram_3, "fsdp", 1), swap(after(gram_far, got), "fsdp", 1)]

    gram, turned = whole_gram(after(token, leave_2), x, pieces)
    moved = residual(stay, got, gram)
    code_a = code(second_code_kernel, after(code_a, moved), got_a, outer_a, WEIGHT["code_3"])
    code_b = code(second_code_kernel, after(code_b, code_a), got_b, outer_b, WEIGHT["code_4"])
    got_a = swap(code_a, "rep", 1)
    got_b = swap(code_b, "rep", 2)

    updated = near_update(
        after(token, moved), (code_a, code_b), (outer_a, outer_b), fetched[:2], (rep_a, rep_b), outer.shape
    )
    mine = [moved] + [swap(moved, "fsdp", 2 * k) for k in range(1, chips)]
    mine = [after(piece, updated[0]) for piece in mine]
    pairs = [(piece, swap(piece, "fsdp", 1)) for piece in mine]
    result = weight_step(token, turned, w, pairs, range(chips), rate, None)
    outers = far_update(after(token, result), (got_a, got_b), fetched[2:], updated)
    return result, *outers


def plain_outer(outer, moment, rep_rows):
    replica_rows = rep_rows.astype(F32)
    delta = lax.psum(outer - replica_rows, "rep") / lax.axis_size("rep")
    new_moment = momentum_coef * moment + delta
    new_outer = outer - outer_rate * (delta + momentum_coef * new_moment)
    mixed = merge_keep * replica_rows + (1.0 - merge_keep) * new_outer
    return new_outer, new_moment, mixed.astype(BF16)


def plain_inner(x, t, w):
    scale = (x.shape[1] * lax.axis_size("fsdp")) ** -0.5
    for _ in range(INNER):
        part = jnp.dot(x, w.astype(BF16), preferred_element_type=F32).astype(BF16)
        predicted = lax.psum_scatter(part, "fsdp", scatter_dimension=0, tiled=True).astype(F32) * scale
        errors = lax.all_gather((predicted - t.astype(F32)).astype(BF16), "fsdp", axis=0, tiled=True)
        gradient = lax.dot_general(x, errors, (((0,), (0,)), ((), ())), preferred_element_type=F32)
        w = w - inner_rate * scale * gradient
    return w


def local(tokens, targets, inner_weights, outer_weights, outer_momentum, replica_weights):
    x, t, w, rep_rows = tokens[0], targets[0], inner_weights[0], replica_weights[0]
    tiles = x.shape[0] // LANES
    if (
        lax.axis_size("fsdp") == 8
        and lax.axis_size("rep") == 4
        and w.shape[1] == 8 * LANES
        and x.shape[0] % LANES == 0
        and tiles * (tiles + 1) % 4 == 0
        and rep_rows.shape[0] % (4 * PART) == 0
    ):
        new_inner, new_outer, new_moment, merged = both(x, t, w, outer_weights, outer_momentum, rep_rows)
    else:
        new_outer, new_moment, merged = plain_outer(outer_weights, outer_momentum, rep_rows)
        new_inner = plain_inner(x, t, w)
    return new_inner[None], new_outer, new_moment, merged[None]


def solution(mesh):
    placed = (
        P("rep", None, "fsdp"),
        P("rep", "fsdp", None),
        P("rep", "fsdp", None),
        P("fsdp", None),
        P("fsdp", None),
        P("rep", "fsdp", None),
    )
    return jax.shard_map(
        local,
        mesh=mesh,
        in_specs=placed,
        out_specs=(
            P("rep", "fsdp", None),
            P("fsdp", None),
            P("fsdp", None),
            P("rep", "fsdp", None),
        ),
        check_vma=False,
    )
```

```python
import functools

import jax
import jax.numpy as jnp
from jax import lax
from jax.experimental import pallas as pl
from jax.experimental.pallas import tpu as pltpu
from jax.sharding import PartitionSpec as P

INNER = 2

inner_rate = 0.5
momentum_coef = 0.9
outer_rate = 0.7
merge_keep = 0.5

F32 = jnp.float32
BF16 = jnp.bfloat16
LANES = 128
SPAN = 2 * LANES
MIB = 1 << 20
US = 1150000000

CODE_SCALE = 2.0**60
CODE_LEAST = 2.0**-30
CODE_CUT = 2.0**20


WEIGHT = {
    "prefetch": 0,
    "opening": 1,
    "fetch": 0,
    "add_1": 0,
    "add_2": 20,
    "add_3": 20,
    "fold_1": 20,
    "fold_2": 8,
    "code_1": 0,
    "code_2": 0,
    "code_3": 0,
    "code_4": 0,
    "whole_gram": 0,
    "residual": 4,
    "near_update": 20,
    "weight_step": 0,
    "far_update": 0,
}


def encode(total, outer_rows, count):
    away = count * outer_rows - total
    held = jnp.where(jnp.abs(total) < CODE_LEAST, CODE_LEAST, total) * CODE_SCALE
    return jnp.where(jnp.abs(total) < jnp.abs(away), held, away).astype(BF16)


def decode_total(code, outer_rows, count):
    code = code.astype(F32)
    return jnp.where(jnp.abs(code) > CODE_CUT, code * (1.0 / CODE_SCALE), count * outer_rows - code)


def decode_away(code, outer_rows, count):
    code = code.astype(F32)
    return jnp.where(jnp.abs(code) > CODE_CUT, count * outer_rows - code * (1.0 / CODE_SCALE), code)


def swap(value, axis, flip):
    count = lax.axis_size(axis)
    return lax.ppermute(value, axis, [(i, i ^ flip) for i in range(count)])


VMEM = pl.BlockSpec(memory_space=pltpu.VMEM)
HBM = pl.BlockSpec(memory_space=pl.ANY)
SMEM = pl.BlockSpec(memory_space=pltpu.SMEM)


def in_hbm(value):
    return pltpu.with_memory_space_constraint(value, pltpu.HBM)


def near(shape, dtype):
    return pltpu.VMEM(tuple(shape), dtype)


def far(shape, dtype):
    return pltpu.HBM(tuple(shape), dtype)


def run(kernel, outs, ins, copies, scratch=(), weight=0, mib=8, aliases=None, name="kernel"):
    specs = [spec for _, spec in ins]
    return pl.pallas_call(
        kernel,
        out_shape=tuple(outs),
        in_specs=specs,
        out_specs=tuple(VMEM if out.memory_space == pltpu.VMEM else HBM for out in outs),
        scratch_shapes=list(scratch) + ([pltpu.SemaphoreType.DMA((copies,))] if copies else []),
        input_output_aliases=aliases or {},
        compiler_params=pltpu.CompilerParams(vmem_limit_bytes=mib * MIB),
        cost_estimate=pl.CostEstimate(flops=weight * US, bytes_accessed=1000, transcendentals=0),
        name=name,
    )(*[value for value, _ in ins])


def rows_at(block, size):
    return pl.ds(pl.multiple_of(block * size, size), size)


CORE, SHARD, CHIP_BIT_0, CHIP_BIT_1, KEEP_A, SEND_A, KEEP_B, SEND_B, CHIP = range(9)


def here(entry):
    shard, rep = lax.axis_index("fsdp"), lax.axis_index("rep")
    bit_a, bit_b = rep & 1, (rep >> 1) & 1
    table = (
        shard & 1, shard, (shard >> 1) & 1, (shard >> 2) & 1,
        bit_a, 1 - bit_a, 2 + bit_b, 3 - bit_b, shard >> 1,
    )
    return table[entry]


def reversed_bits(value, bits):
    return sum(((value >> bit) & 1) << (bits - 1 - bit) for bit in range(bits))


def open_kernel(
    scale, rate, x_ref, t_ref, w_ref, rep_ref, gram_keep, gram_send, x_out, w_out, first_a, first_b, keep_ref, *refs
):
    sends, (acc_ref, t_held, sems) = refs[:-3], refs[-3:]
    steps = keep_ref.shape[0]
    each_send = steps // len(sends)
    bits = steps.bit_length() - 1
    quarter = first_a.shape[0]
    depth = w_ref.shape[0]
    cut = depth // CUTS
    core = here(CORE)
    copy_x = pltpu.make_async_copy(x_ref, x_out, sems.at[0])
    copies_w = [
        pltpu.make_async_copy(w_ref.at[pl.ds(k * cut, cut)], w_out.at[pl.ds(k * cut, cut)], sems.at[4 + k])
        for k in range(CUTS)
    ]
    others = [
        pltpu.make_async_copy(t_ref, t_held, sems.at[1]),
        pltpu.make_async_copy(rep_ref.at[rows_at(here(SEND_A), quarter)], first_a, sems.at[2]),
        pltpu.make_async_copy(rep_ref.at[rows_at(here(SEND_B), quarter)], first_b, sems.at[3]),
    ]
    for copy in (copy_x, *copies_w, *others):
        copy.start()
    copy_x.wait()
    x = x_out[...]
    gram = lax.dot_general(x, x, (((1,), (1,)), ((), ())), preferred_element_type=F32) * (rate * scale * scale)
    tiles = x.shape[0] // LANES
    pairs = [(i, j) for i in range(tiles) for j in range(i, tiles)]
    each = len(pairs) // 2
    for place, (i, j) in enumerate(pairs):
        part = gram[i * LANES : (i + 1) * LANES, j * LANES : (j + 1) * LANES].astype(BF16)
        side, spot = place // each, place % each
        rows = pl.ds(spot * LANES, LANES)

        @pl.when(core == side)
        def _():
            gram_keep[rows, :] = part

        @pl.when(core != side)
        def _():
            gram_send[rows, :] = part

    for k in range(CUTS):
        copies_w[k].wait()
        rows = pl.ds(k * cut, cut)
        part = jnp.dot(x_out[:, rows], w_out[rows, :].astype(BF16), preferred_element_type=F32)
        acc_ref[...] = part if k == 0 else acc_ref[...] + part
    others[0].wait()
    own = t_held.shape[0]
    rows = rows_at(here(SHARD), own)
    acc_ref[rows, :] = acc_ref[rows, :] - t_held[...].astype(F32) * (1.0 / scale)
    for j in range(steps):
        low = reversed_bits(j, bits) * SPAN
        for side in range(2):
            columns = slice(low + side * LANES, low + (side + 1) * LANES)

            @pl.when(core == side)
            def _():
                keep_ref[j] = (acc_ref[:, columns] * scale).astype(BF16)

            @pl.when(core != side)
            def _():
                sends[j // each_send][j % each_send] = (acc_ref[:, columns] * scale).astype(BF16)

    for copy in others[1:]:
        copy.wait()


CUTS = 2
SENDS = 2


def opening(x, t, w, rep_rows, scale, rate):
    tokens, depth = x.shape
    tiles = tokens // LANES
    each = tiles * (tiles + 1) // 4 * LANES
    quarter = (rep_rows.shape[0] // 4, rep_rows.shape[1])
    steps = w.shape[1] // SPAN
    return run(
        functools.partial(open_kernel, scale, rate),
        [near((each, LANES), BF16)] * 2
        + [near(x.shape, BF16), near(w.shape, F32)]
        + [near(quarter, BF16)] * 2
        + [near((steps, tokens, LANES), BF16)]
        + [near((steps // SENDS, tokens, LANES), BF16)] * SENDS,
        [(in_hbm(value), HBM) for value in (x, t, w, rep_rows)],
        4 + CUTS,
        scratch=[pltpu.VMEM((tokens, w.shape[1]), F32), pltpu.VMEM(t.shape, BF16)],
        weight=WEIGHT["opening"],
        name="opening",
    )


def prefetch_kernel(
    token_ref, outer_ref, moment_ref, rep_ref,
    moment_a, moment_b, far_outer_a, far_outer_b, far_moment_a, far_moment_b, far_rep_a, far_rep_b, sems,
):
    del token_ref
    quarter = moment_a.shape[0]
    copies = []
    for k, (source, entry, target) in enumerate(
        [
            (moment_ref, KEEP_A, moment_a),
            (moment_ref, KEEP_B, moment_b),
            (outer_ref, SEND_A, far_outer_a),
            (outer_ref, SEND_B, far_outer_b),
            (moment_ref, SEND_A, far_moment_a),
            (moment_ref, SEND_B, far_moment_b),
            (rep_ref, SEND_A, far_rep_a),
            (rep_ref, SEND_B, far_rep_b),
        ]
    ):
        copy = pltpu.make_async_copy(source.at[rows_at(here(entry), quarter)], target, sems.at[k])
        copy.start()
        copies.append(copy)
    for copy in copies:
        copy.wait()


def prefetch(token, outer, moment, rep_rows):
    quarter = (outer.shape[0] // 4, outer.shape[1])
    return run(
        prefetch_kernel,
        [near(quarter, F32)] * 6 + [near(quarter, BF16)] * 2,
        [(token, HBM)] + [(in_hbm(value), HBM) for value in (outer, moment, rep_rows)],
        8,
        weight=WEIGHT["prefetch"],
        name="prefetch",
    )


def fetch_kernel(token_ref, rep_ref, outer_ref, rep_a, rep_b, outer_a, outer_b, sems):
    del token_ref
    quarter = rep_a.shape[0]
    copies = []
    for k, (source, entry, target) in enumerate(
        [(rep_ref, KEEP_A, rep_a), (rep_ref, KEEP_B, rep_b), (outer_ref, KEEP_A, outer_a), (outer_ref, KEEP_B, outer_b)]
    ):
        copy = pltpu.make_async_copy(source.at[rows_at(here(entry), quarter)], target, sems.at[k])
        copy.start()
        copies.append(copy)
    for copy in copies:
        copy.wait()


def fetch(token, rep_rows, outer):
    quarter = (rep_rows.shape[0] // 4, rep_rows.shape[1])
    return run(
        fetch_kernel,
        [near(quarter, BF16)] * 2 + [near(quarter, F32)] * 2,
        [(token, HBM), (in_hbm(rep_rows), HBM), (in_hbm(outer), HBM)],
        4,
        weight=WEIGHT["fetch"],
        name="fetch",
    )


def fold_kernel(entry, token_ref, own_ref, *refs):
    gots, leave_ref, stay_ref = refs[:-2], refs[-2], refs[-1]
    size = stay_ref.shape[0]
    each = own_ref.shape[0] // len(gots)

    def total(place):
        got = gots[place // each]
        got = got[...] if each == 1 and len(got.shape) == 2 else got[place % each]
        return own_ref[place].astype(F32) + got.astype(F32)

    for side in range(2):

        @pl.when(here(entry) == side)
        def _():
            for k in range(size):
                leave_ref[k] = total((1 - side) * size + k).astype(BF16)
                stay_ref[k] = total(side * size + k)


def fold(token, own, gots, entry, weight):
    size, tokens, width = own.shape
    shape = (size // 2, tokens, width)
    return run(
        functools.partial(fold_kernel, entry),
        [near(shape, BF16), near(shape, F32)],
        [(token, HBM), (own, VMEM)] + [(got, VMEM) for got in gots],
        0,
        weight=weight,
        name="fold",
    )


def add_kernel(own_ref, got_ref, out_ref):
    out_ref[...] = (own_ref[...].astype(F32) + got_ref[...].astype(F32)).astype(BF16)


def add(own, got, weight):
    return run(
        add_kernel,
        [near(own.shape, BF16)],
        [(own, VMEM), (got, VMEM)],
        0,
        weight=weight,
        name="add",
    )[0]


def whole_gram_kernel(token_ref, x_ref, near_ref, far_ref, other_near, other_far, out_ref, turned_ref, pack_ref):
    rows = near_ref.shape[0]
    core, side = here(CORE), here(CHIP_BIT_0)
    for ref, half, part in (
        (near_ref, core, side),
        (far_ref, core, 1 - side),
        (other_near, 1 - core, side),
        (other_far, 1 - core, 1 - side),
    ):
        pack_ref[rows_at(2 * half + part, rows), :] = ref[...]
    tiles = out_ref.shape[0] // LANES
    pairs = [(i, j) for i in range(tiles) for j in range(i, tiles)]
    for place, (i, j) in enumerate(pairs):
        part = pack_ref[place * LANES : (place + 1) * LANES, :]
        out_ref[i * LANES : (i + 1) * LANES, j * LANES : (j + 1) * LANES] = part
        if i != j:
            out_ref[j * LANES : (j + 1) * LANES, i * LANES : (i + 1) * LANES] = part.T
    turned_ref[...] = x_ref[...].T


def whole_gram(token, x, pieces):
    tokens, depth = x.shape
    return run(
        whole_gram_kernel,
        [near((tokens, tokens), BF16), near((depth, tokens), BF16)],
        [(token, HBM), (x, VMEM)] + [(piece, VMEM) for piece in pieces],
        0,
        scratch=[pltpu.VMEM((4 * pieces[0].shape[0], LANES), BF16)],
        weight=WEIGHT["whole_gram"],
        name="whole_gram",
    )


def residual_kernel(own_ref, got_ref, gram_ref, out_ref):
    error = own_ref[0] + got_ref[0].astype(F32)
    moved = jnp.dot(gram_ref[...], error.astype(BF16), preferred_element_type=F32)
    out_ref[...] = (2.0 * error - moved).astype(BF16)


def residual(own, got, gram):
    _, tokens, width = own.shape
    return run(
        residual_kernel,
        [near((tokens, width), BF16)],
        [(own, VMEM), (got, VMEM), (gram, VMEM)],
        0,
        weight=WEIGHT["residual"],
        name="residual",
    )[0]


STEP_CUTS = 4


def step_kernel(rate, places, token_ref, turned_ref, w_ref, *refs):
    count = len(places)
    pieces = refs[: 2 * count]
    out_ref, pair_ref, buffer_ref, sems = refs[-4:]
    first = here(CORE) == 0
    copies = []
    depth = w_ref.shape[0]
    cut = depth // STEP_CUTS
    for k, flip in enumerate(places):
        mine, other = pieces[2 * k][...], pieces[2 * k + 1][...]
        pair_ref[k, :, :LANES] = jnp.where(first, mine, other)
        pair_ref[k, :, LANES:] = jnp.where(first, other, mine)
        place = jnp.bitwise_xor(here(CHIP), flip)
        columns = pl.ds(pl.multiple_of(place * SPAN, SPAN), SPAN)
        for part in range(STEP_CUTS):
            rows = pl.ds(part * cut, cut)
            grad = jnp.dot(turned_ref[rows, :], pair_ref[k], preferred_element_type=F32)
            buffer_ref[k, rows, :] = w_ref[rows, columns] - rate * grad
            copy = pltpu.make_async_copy(
                buffer_ref.at[k, rows], out_ref.at[rows, columns], sems.at[STEP_CUTS * k + part]
            )
            copy.start()
            copies.append(copy)
    for copy in copies:
        copy.wait()


def weight_step(token, turned, w, pairs, places, rate, before):
    depth, tokens = turned.shape
    count = len(pairs)
    flat = [piece for pair in pairs for piece in pair]
    ins = [(token, HBM), (turned, VMEM), (w, VMEM)] + [(piece, VMEM) for piece in flat]
    aliases = {}
    if before is not None:
        aliases = {len(ins): 0}
        ins.append((before, HBM))
    return run(
        functools.partial(step_kernel, rate, tuple(places)),
        [far(w.shape, F32)],
        ins,
        STEP_CUTS * count,
        scratch=[pltpu.VMEM((count, tokens, SPAN), BF16), pltpu.VMEM((count, depth, SPAN), F32)],
        aliases=aliases,
        weight=WEIGHT["weight_step"],
        name="weight_step",
    )[0]


def first_code_kernel(rep_ref, got_ref, outer_ref, code_ref):
    total = rep_ref[...].astype(F32) + got_ref[...].astype(F32)
    code_ref[...] = encode(total, outer_ref[...], 2.0)


def second_code_kernel(own_ref, got_ref, outer_ref, code_ref):
    outer = outer_ref[...]
    total = decode_total(own_ref[...], outer, 2.0) + decode_total(got_ref[...], outer, 2.0)
    code_ref[...] = encode(total, outer, 4.0)


def code(kernel, own, got, outer_rows, weight):
    return run(
        kernel,
        [near(own.shape, BF16)],
        [(own, VMEM), (got, VMEM), (outer_rows, VMEM)],
        0,
        weight=weight,
        name="code",
    )[0]


PART = 128


def update_rows(entries, codes, outers, moments, reps, outs, buffers, sems, ready):
    size = codes[0].shape[0]
    copies = []
    part = min(PART, size)
    for half in range(2):
        for cut in range(size // part):
            spot = half * (size // part) + cut
            rows = pl.ds(cut * part, part)
            held = pl.ds(spot * part, part)
            if cut == 0:
                ready(half)
            outer = outers[half][rows, :]
            delta = decode_away(codes[half][rows, :], outer, 4.0) * 0.25
            moment = momentum_coef * moments[half][rows, :] + delta
            new_outer = outer - outer_rate * (delta + momentum_coef * moment)
            mixed = merge_keep * reps[half][rows, :].astype(F32) + (1.0 - merge_keep) * new_outer
            for k, value in enumerate((new_outer, moment, mixed.astype(BF16))):
                buffers[k][held, :] = value
                target = rows_at(here(entries[half]) * (size // part) + cut, part)
                copy = pltpu.make_async_copy(buffers[k].at[held], outs[k].at[target], sems.at[3 * spot + k])
                copy.start()
                copies.append(copy)
    for copy in copies:
        copy.wait()


def near_update_kernel(
    token_ref, code_a, code_b, outer_a, outer_b, moment_a, moment_b, rep_a, rep_b,
    new_outer, new_moment, merged, buffer_outer, buffer_moment, buffer_merged, sems,
):
    del token_ref
    update_rows(
        (KEEP_A, KEEP_B), (code_a, code_b), (outer_a, outer_b), (moment_a, moment_b), (rep_a, rep_b),
        (new_outer, new_moment, merged), (buffer_outer, buffer_moment, buffer_merged), sems,
        lambda half: None,
    )


def far_update_kernel(
    token_ref, code_a, code_b, outer_a, outer_b, moment_a, moment_b, rep_a, rep_b, held_a, held_b, held_c,
    new_outer, new_moment, merged, buffer_outer, buffer_moment, buffer_merged, sems,
):
    del held_a, held_b, held_c
    update_rows(
        (SEND_A, SEND_B), (code_a, code_b), (outer_a, outer_b), (moment_a, moment_b), (rep_a, rep_b),
        (new_outer, new_moment, merged), (buffer_outer, buffer_moment, buffer_merged), sems,
        lambda half: None,
    )


def update_scratch(size, width):
    return [pltpu.VMEM((2 * size, width), dtype) for dtype in (F32, F32, BF16)]


def near_update(token, codes, outers, moments, reps, full):
    size, width = codes[0].shape
    return run(
        near_update_kernel,
        [far(full, F32), far(full, F32), far(full, BF16)],
        [(token, HBM)] + [(value, VMEM) for value in (*codes, *outers, *moments, *reps)],
        6 * max(size // PART, 1),
        scratch=update_scratch(size, width),
        mib=16,
        weight=WEIGHT["near_update"],
        name="near_update",
    )


def far_update(token, codes, fetched, before):
    size, width = codes[0].shape
    outs = [far(value.shape, value.dtype) for value in before]
    ins = [(token, HBM)] + [(value, VMEM) for value in (*codes, *fetched)]
    return run(
        far_update_kernel,
        outs,
        ins + [(value, HBM) for value in before],
        6 * max(size // PART, 1),
        scratch=update_scratch(size, width),
        mib=16,
        aliases={len(ins) + k: k for k in range(3)},
        weight=WEIGHT["far_update"],
        name="far_update",
    )


def after(value, *others):
    return lax.optimization_barrier((value, *others))[0]


def both(x, t, w, outer, moment, rep_rows):
    shards = lax.axis_size("fsdp")
    chips = shards // 2
    scale = (x.shape[1] * shards) ** -0.5
    rate = inner_rate * scale
    token = t

    gram_keep, gram_send, x, w, first_a, first_b, keep, *sends = opening(x, t, w, rep_rows, scale, inner_rate)
    gram_got = swap(gram_send, "fsdp", 1)
    got = [swap(send, "fsdp", 1) for send in sends]
    got_a, got_b = swap(first_a, "rep", 1), swap(first_b, "rep", 2)
    halves = (2, gram_keep.shape[0] // 2, LANES)
    gram_leave, gram_stay = fold(
        token, gram_keep.reshape(halves), [gram_got.reshape(halves)], CHIP_BIT_0, WEIGHT["add_1"]
    )
    gram_got = swap(gram_leave[0], "fsdp", 2)

    leave_1, stay = fold(after(token, gram_leave), keep, got, CHIP_BIT_0, WEIGHT["fold_1"])
    got = swap(leave_1, "fsdp", 2)
    rep_a, rep_b, outer_a, outer_b = fetch(after(token, leave_1), rep_rows, outer)
    gram_2 = add(after(gram_stay, rep_a)[0], gram_got, WEIGHT["add_2"])
    gram_got = swap(gram_2, "fsdp", 4)

    fetched = prefetch(after(token, gram_2), outer, moment, rep_rows)
    leave_2, stay = fold(token, after(stay, gram_2, fetched[0]), [got], CHIP_BIT_1, WEIGHT["fold_2"])
    got = swap(leave_2, "fsdp", 4)
    code_a = code(first_code_kernel, after(rep_a, leave_2), got_a, outer_a, WEIGHT["code_1"])
    code_b = code(first_code_kernel, after(rep_b, code_a), got_b, outer_b, WEIGHT["code_2"])
    got_a = swap(code_a, "rep", 2)
    got_b = swap(code_b, "rep", 1)

    gram_3 = add(after(gram_2, leave_2), gram_got, WEIGHT["add_3"])
    gram_far = swap(gram_3, "fsdp", 2)
    pieces = [gram_3, gram_far, swap(gram_3, "fsdp", 1), swap(after(gram_far, got), "fsdp", 1)]

    gram, turned = whole_gram(after(token, leave_2), x, pieces)
    moved = residual(stay, got, gram)
    code_a = code(second_code_kernel, after(code_a, moved), got_a, outer_a, WEIGHT["code_3"])
    code_b = code(second_code_kernel, after(code_b, code_a), got_b, outer_b, WEIGHT["code_4"])
    got_a = swap(code_a, "rep", 1)
    got_b = swap(code_b, "rep", 2)

    updated = near_update(
        after(token, moved), (code_a, code_b), (outer_a, outer_b), fetched[:2], (rep_a, rep_b), outer.shape
    )
    moved_by = {k: swap(moved, "fsdp", 2 * k) for k in (1, 3, 2)}
    mine = [moved] + [moved_by[k] for k in range(1, chips)]
    mine = [after(piece, updated[0]) for piece in mine]
    pairs = [(piece, swap(piece, "fsdp", 1)) for piece in mine]
    result = weight_step(token, turned, w, pairs, range(chips), rate, None)
    outers = far_update(after(token, result), (got_a, got_b), fetched[2:], updated)
    return result, *outers


def plain_outer(outer, moment, rep_rows):
    replica_rows = rep_rows.astype(F32)
    delta = lax.psum(outer - replica_rows, "rep") / lax.axis_size("rep")
    new_moment = momentum_coef * moment + delta
    new_outer = outer - outer_rate * (delta + momentum_coef * new_moment)
    mixed = merge_keep * replica_rows + (1.0 - merge_keep) * new_outer
    return new_outer, new_moment, mixed.astype(BF16)


def plain_inner(x, t, w):
    scale = (x.shape[1] * lax.axis_size("fsdp")) ** -0.5
    for _ in range(INNER):
        part = jnp.dot(x, w.astype(BF16), preferred_element_type=F32).astype(BF16)
        predicted = lax.psum_scatter(part, "fsdp", scatter_dimension=0, tiled=True).astype(F32) * scale
        errors = lax.all_gather((predicted - t.astype(F32)).astype(BF16), "fsdp", axis=0, tiled=True)
        gradient = lax.dot_general(x, errors, (((0,), (0,)), ((), ())), preferred_element_type=F32)
        w = w - inner_rate * scale * gradient
    return w


def local(tokens, targets, inner_weights, outer_weights, outer_momentum, replica_weights):
    x, t, w, rep_rows = tokens[0], targets[0], inner_weights[0], replica_weights[0]
    tiles = x.shape[0] // LANES
    if (
        lax.axis_size("fsdp") == 8
        and lax.axis_size("rep") == 4
        and w.shape[1] == 8 * LANES
        and x.shape[0] % LANES == 0
        and tiles * (tiles + 1) % 4 == 0
        and rep_rows.shape[0] % (4 * PART) == 0
    ):
        new_inner, new_outer, new_moment, merged = both(x, t, w, outer_weights, outer_momentum, rep_rows)
    else:
        new_outer, new_moment, merged = plain_outer(outer_weights, outer_momentum, rep_rows)
        new_inner = plain_inner(x, t, w)
    return new_inner[None], new_outer, new_moment, merged[None]


def solution(mesh):
    placed = (
        P("rep", None, "fsdp"),
        P("rep", "fsdp", None),
        P("rep", "fsdp", None),
        P("fsdp", None),
        P("fsdp", None),
        P("rep", "fsdp", None),
    )
    return jax.shard_map(
        local,
        mesh=mesh,
        in_specs=placed,
        out_specs=(
            P("rep", "fsdp", None),
            P("fsdp", None),
            P("fsdp", None),
            P("rep", "fsdp", None),
        ),
        check_vma=False,
    )
```
